512 devices in a mesh: gx: 8 (over z), gy: 8 (over y), gz: 8 (over x, core).
Axes of the slice: x: 4, y: 8, z: 8, core: 2. Of those that a mesh axis runs over, the one named last changes fastest.
Arguments:
- hidden_states: bfloat16 [512, 8192], P(('gx', 'gy'), 'gz'), may hold values from -17 to 17
- weight: bfloat16 [8192, 65536], P('gz', ('gx', 'gy')), may hold values from -1 to 1
- targets: int32 [512], replicated, may hold values from 0 to 65535
- upstream: bfloat16 [512], replicated, may hold values from 8 to 64
Outputs:
- grad_hidden: bfloat16 [512, 8192], P(('gx', 'gy'), 'gz')
- grad_weight: bfloat16 [8192, 65536], P('gz', ('gx', 'gy'))
The draws below stay inside these ranges and needn't reach their ends.
All inputs are finite; a program needn't handle non-finite values.
Results may differ from the reference program's by a relative error of at most 0.009.
Values may be sent and summed in bfloat16 or wider, within the bound.
A program may use at most 64 MiB of HBM per device.

```python
import math
import jax
import jax.numpy as jnp
import numpy as np

D = 8192
TOKENS = 512
VOCAB = 65536


def column_scales(key):
    position = jnp.arange(VOCAB, dtype=jnp.float32) / max(VOCAB - 1, 1)
    rough = jnp.exp(jax.random.uniform(jax.random.fold_in(key, 102), (VOCAB,), jnp.float32, -0.17, 0.17))
    return (2.2 + 0.8 * position) * rough / math.sqrt(D)


def pick_columns(key):
    order = jax.random.permutation(jax.random.fold_in(key, 103), VOCAB)
    return order[:12 + TOKENS // 8].astype(jnp.int32)


def pick_vectors(key):
    signs = jax.random.rademacher(jax.random.fold_in(key, 104), (6 + TOKENS // 8, D), jnp.float32)
    alternate = 1.0 - 2.0 * (jnp.arange(D, dtype=jnp.int32) % 2).astype(jnp.float32)
    return jnp.concatenate([signs[:6], signs[:6] * alternate[None, :], signs[6:]], axis=0)


def draw_weight(key, part):
    scales = column_scales(key)
    picks = pick_columns(key)
    vectors = pick_vectors(key)
    key = jax.random.fold_in(key, 3)
    normal_part = jnp.clip(jax.random.normal(jax.random.fold_in(key, 1), (D, VOCAB), jnp.float32), -6.0, 6.0)
    common = jnp.clip(jax.random.normal(jax.random.fold_in(key, 2), (D, 1), jnp.float32), -6.0, 6.0) * (1.5 / math.sqrt(D))
    loading = jax.random.uniform(jax.random.fold_in(key, 4), (1, VOCAB), jnp.float32, 0.7, 1.3)
    values = normal_part * scales[None, :] + common * loading
    values = values.at[:, picks].set(vectors.T * scales[picks][None, :])
    return values.astype(jnp.bfloat16)


def draw_hidden_states(key, part):
    scales = column_scales(key)
    picks = pick_columns(key)
    vectors = pick_vectors(key)
    key = jax.random.fold_in(key, 5)
    values = jnp.clip(jax.random.normal(key, (TOKENS, D), jnp.float32), -6.0, 6.0)
    spread = TOKENS // 8
    aligned = vectors / (D * scales[picks])[:, None]
    strength = jnp.array([68.0, 72.0, 103.0, 132.0, 200.0, 240.0], jnp.float32)
    planted = strength[:, None] * aligned[:6] + (strength - 2.0)[:, None] * aligned[6:12]
    quiet = 0.01 * values[6:6 + spread]
    peaked = 0.01 * values[6 + spread:6 + 2 * spread] + 11.1 * aligned[12:]
    values = values.at[:6].set(planted)
    values = values.at[6:6 + spread].set(quiet)
    values = values.at[6 + spread:6 + 2 * spread].set(peaked)
    return values.astype(jnp.bfloat16)


def plant(values, own_key, least, largest):
    longest = values.shape.index(max(values.shape))
    spots = []
    for shift in (0, 1):
        where = [jax.random.randint(jax.random.fold_in(own_key, axis), (), 0, length) for axis, length in enumerate(values.shape)]
        where[longest] = (where[longest] + shift) % values.shape[longest]
        spots.append(tuple(where))
    return values.at[spots[0]].set(least).at[spots[1]].set(largest)


def rank_bounds(amount, skew):
    portions = [(1 << 20) // math.isqrt(grade ** skew) + 1 for grade in range(1, amount + 1)]
    deviation = 1 + sum(portions) // (1 << 30)
    return np.cumsum(np.array([max(1, weight // deviation) for weight in portions]))


def ranked_ids(rng, dims, number_of, slope):
    table = rank_bounds(number_of, slope)
    ticket = jax.random.randint(jax.random.fold_in(rng, 1), dims, 0, int(table[number_of - 1]))
    rank = jnp.searchsorted(jnp.asarray(table, jnp.int32), ticket, side="right")
    return jax.random.permutation(jax.random.fold_in(rng, 2), number_of)[rank].astype(jnp.int32)


def setup_inputs(seed: int = 0) -> dict:
    arg_keys = jax.random.split(jax.random.key(seed), 5)
    hidden_states = draw_hidden_states(jax.random.fold_in(arg_keys[4], 71), 0)
    weight = draw_weight(jax.random.fold_in(arg_keys[4], 71), 0)
    targets = plant(ranked_ids(arg_keys[2], (TOKENS,), VOCAB, 2), jax.random.fold_in(arg_keys[2], 3), 0, VOCAB - 1).astype(jnp.int32)
    upstream = jnp.clip(jnp.exp(jax.random.uniform(arg_keys[3], (TOKENS,), jnp.float32, math.log(8.0), math.log(64.0))), 8.0, 64.0).astype(jnp.bfloat16)
    return {"hidden_states": hidden_states, "weight": weight, "targets": targets, "upstream": upstream}


def reference(hidden_states, weight, targets, upstream):
    logits = jnp.dot(hidden_states, weight, preferred_element_type=jnp.float32)
    row_peak = jnp.max(logits, axis=1, keepdims=True)
    shifted = jnp.exp(logits - row_peak)
    probability = shifted / jnp.sum(shifted, axis=1, keepdims=True)
    columns = jnp.arange(logits.shape[1], dtype=jnp.int32)
    one_hot = (targets.astype(jnp.int32)[:, None] == columns[None, :]).astype(jnp.float32)
    grad_logits = (upstream.astype(jnp.float32)[:, None] * (probability - one_hot)).astype(jnp.bfloat16)
    grad_hidden = jnp.dot(grad_logits, weight.T, preferred_element_type=jnp.float32).astype(jnp.bfloat16)
    grad_weight = jnp.dot(hidden_states.T, grad_logits, preferred_element_type=jnp.float32).astype(jnp.bfloat16)
    return grad_hidden, grad_weight
```

```python
import functools

import jax
import jax.numpy as jnp
from jax import lax
from jax.experimental import pallas as pl
from jax.experimental.pallas import tpu as pltpu
from jax.sharding import PartitionSpec as P

MESH = pl.DeviceIdType.MESH
F32, BF16, I32 = jnp.float32, jnp.bfloat16, jnp.int32
FAR_FIRST = (4, 3, 5, 2, 6, 1, 7)
GROUP = ((2, 0), (2, 1), (1, 0), (3, 0), (1, 1), (3, 1), (0, 1))


def remote(src, dst, send_sem, recv_sem, device):
    return pltpu.make_async_remote_copy(
        src_ref=src, dst_ref=dst, send_sem=send_sem, recv_sem=recv_sem, device_id=device, device_id_type=MESH
    )


def upper_rows(shape):
    return lax.broadcasted_iota(I32, shape, 0) < 4


def pack(a):
    q = [a[:, 256 * k : 256 * (k + 1)] for k in range(4)]
    t = [pltpu.roll(x, 4, 0) for x in q]
    first = upper_rows((8, 256))
    low = jnp.concatenate([jnp.where(first, q[0], t[1]), jnp.where(first, q[2], t[3])], axis=0)
    high = jnp.concatenate([jnp.where(first, t[0], q[1]), jnp.where(first, t[2], q[3])], axis=0)
    return low, high


def unpack(low, high):
    first = upper_rows((8, 256))
    parts = []
    for k in range(2):
        a, c = low[8 * k : 8 * k + 8], high[8 * k : 8 * k + 8]
        parts.append(jnp.where(first, a, pltpu.roll(c, 4, 0)))
        parts.append(jnp.where(first, pltpu.roll(a, 4, 0), c))
    return jnp.concatenate(parts, axis=1)


def rows_of(*rows):
    sub = lax.broadcasted_iota(I32, (8, 128), 0)
    out = jnp.zeros((8, 128), F32)
    for k, row in enumerate(rows):
        out = jnp.where(sub == k, jnp.broadcast_to(row, (8, 128)), out)
    return out


def combine(stats):
    peaks = [stats[k, 0:1, :] for k in range(stats.shape[0])]
    peak = functools.reduce(jnp.maximum, peaks)
    scale = [jnp.exp(p - peak) for p in peaks]
    total = sum(stats[k, 1:2, :] * scale[k] for k in range(stats.shape[0]))
    chosen = sum(stats[k, 2:3, :] * scale[k] for k in range(stats.shape[0]))
    return peak, total, chosen


def kernel(
    h_ref, w_hbm, tgt_ref, up_ref, gh_ref, gw_hbm,
    w, hid, a1s, a1r, keep, cs, cr, xs, xr, e_all, g, p, r1, s2, r2, gwv,
    own_col, stat_col, st_a, st_b, st_c, t_col,
    w_sem, gw_sem, a1_ss, a1_rs, a2_ss, a2_rs, c_ss, c_rs, x_ss, x_rs,
    e_ss, e_rs, sa_ss, sa_rs, sb_ss, sb_rs, sc_ss, sc_rs, d1_ss, d1_rs, d2_ss, d2_rs,
):
    z, y, gz = lax.axis_index("gx"), lax.axis_index("gy"), lax.axis_index("gz")
    xx, core = gz // 2, gz % 2
    vocab = w.shape[1]
    zp, yp = z // 2, y // 2
    me = (z, y)

    def along(kind, d):
        return (z, (y + d) % 8, gz) if kind == 0 else ((z + d) % 8, y, gz)

    def member(dx, flip):
        c = 1 - core if flip else core
        return ((xx + dx) % 4) * 2 + c

    load_w = pltpu.make_async_copy(w_hbm, w, w_sem)
    load_w.start()

    barrier = pltpu.get_barrier_semaphore()
    for d in FAR_FIRST:
        for kind in (0, 1):
            pl.semaphore_signal(barrier, inc=1, device_id=along(kind, d), device_id_type=MESH)
    for dx, flip in GROUP:
        pl.semaphore_signal(barrier, inc=1, device_id=(z, y, member(dx, flip)), device_id_type=MESH)

    low, high = pack(h_ref[...].astype(F32))
    a1s[0] = low.astype(BF16)
    a1s[1] = high.astype(BF16)
    a1r[0, y] = low.astype(BF16)
    a1r[1, z] = high.astype(BF16)

    k = lax.broadcasted_iota(I32, (128, 512), 0)
    t = lax.broadcasted_iota(I32, (128, 512), 1)
    block = 2 * (k >> 4) + xx // 2
    other = (xx % 2) * 4 + ((k >> 2) & 3)
    zt = jnp.where(core == 0, block, other)
    yt = jnp.where(core == 0, other, block)
    token = zt * 64 + yt * 8 + core * 4 + (k & 3)
    select = jnp.where((token == t) & (k < 64), 1.0, 0.0).astype(BF16)
    tgt = tgt_ref[...]
    sub = lax.broadcasted_iota(I32, (128, 512), 0)
    values = jnp.where(sub == 0, jnp.broadcast_to((tgt >> 8).astype(F32), (128, 512)), 0.0)
    values = jnp.where(sub == 1, jnp.broadcast_to((tgt & 255).astype(F32), (128, 512)), values)
    values = jnp.where(sub == 2, jnp.broadcast_to(up_ref[...].astype(F32), (128, 512)), values).astype(BF16)
    contract = (((1,), (1,)), ((), ()))
    own_col[...] = lax.dot_general(select, values, contract, preferred_element_type=F32)
    own_row = lax.dot_general(values, select, contract, preferred_element_type=F32)
    tgt_row = own_row[0:1, :] * 256.0 + own_row[1:2, :]
    up_row = own_row[2:3, :]
    stat_col[...] = jnp.zeros((128, 128), F32)

    pl.semaphore_wait(barrier, 21)

    sends = []
    for d in FAR_FIRST:
        for kind in (0, 1):
            c = remote(a1s.at[kind], a1r.at[kind, me[1 - kind]], a1_ss.at[kind, d], a1_rs.at[kind, me[1 - kind]], along(kind, d))
            c.start()
            sends.append(c)

    def arrived(dst, sem, peer):
        remote(dst, dst, w_sem, sem, peer).wait_recv()

    for kind in (0, 1):
        mine = me[1 - kind]
        for d in range(1, 8):
            src = (mine + d) % 8
            arrived(a1r.at[kind, src], a1_rs.at[kind, src], along(kind, 1))
        for b in range(2):
            rows = [
                unpack(a1r[kind, 4 * b + 2 * q].astype(F32), a1r[kind, 4 * b + 2 * q + 1].astype(F32)) for q in range(2)
            ]
            hid[kind, me[kind], 16 * b : 16 * b + 16, :] = jnp.concatenate(rows, axis=0).astype(BF16)
        for d in (1, 7, 2, 6, 3, 5, 4):
            slot = hid.at[kind, me[kind]]
            c = remote(slot, slot, a2_ss.at[kind, d], a2_rs.at[kind, me[kind]], along(1 - kind, d))
            c.start()
            sends.append(c)

    load_w.wait()

    def shift(s, parity):
        return (0, 2 * parity + 3, 5 - 2 * parity, 2)[s]

    def pair_of(kind, s):
        return (zp + shift(s, z % 2)) % 4 if kind == 0 else (yp + shift(s, y % 2)) % 4

    def own_pair(s):
        return jnp.where(core == 0, pair_of(0, s), pair_of(1, s))

    def other_pair(s):
        return jnp.where(core == 0, pair_of(1, s), pair_of(0, s))

    sibling = (z, y, member(0, 1))

    def multiply(s):
        for kind in (0, 1):
            pair = pair_of(kind, s)
            if s == 0:
                chunks = [4 * pair + 1 - me[kind]]
            else:
                chunks = [2 * pair, 2 * pair + 1]
            for q in chunks:
                arrived(hid.at[kind, q], a2_rs.at[kind, q], along(1 - kind, 1))
        mine, others = own_pair(s), other_pair(s)

        def tile(n, _):
            lanes = pl.ds(pl.multiple_of(n * 256, 256), 256)
            lhs = jnp.concatenate(
                [hid[core, pl.ds(2 * mine, 2)].reshape(64, 1024), hid[1 - core, pl.ds(2 * others, 2)].reshape(64, 1024)],
                axis=0,
            )
            part = jnp.dot(lhs, w[:, lanes], preferred_element_type=F32)
            keep[s, :, lanes] = part[:64]
            cs[s, :, lanes] = part[64:]
            return 0

        lax.fori_loop(0, 4, tile, 0)
        c = remote(cs.at[s], cr.at[s], c_ss.at[s], c_rs.at[s], sibling)
        c.start()
        sends.append(c)

    def pass_on(s):
        arrived(cr.at[s], c_rs.at[s], sibling)
        xs[s] = keep[s] + cr[s]
        for dx in (2, 1, 3):
            to = (xx + dx) % 4
            c = remote(
                xs.at[s, pl.ds(pl.multiple_of(to * 16, 16), 16)], xr.at[s, dx - 1], x_ss.at[s, dx - 1], x_rs.at[s, dx - 1],
                (z, y, member(dx, 0)),
            )
            c.start()
            sends.append(c)

    def finish(s):
        for dx in (2, 1, 3):
            arrived(xr.at[s, dx - 1], x_rs.at[s, dx - 1], sibling)
        pair = own_pair(s)
        logits = xs[s, pl.ds(pl.multiple_of(xx * 16, 16), 16), :] + xr[s, 0] + xr[s, 1] + xr[s, 2]
        rows = pl.ds(pl.multiple_of(pair * 16, 16), 16)
        info = own_col[rows, :]
        target = info[:, 0:1] * 256.0 + info[:, 1:2]
        column = lax.broadcasted_iota(I32, (16, vocab), 1) + (z * 8 + y) * vocab
        hit = column.astype(F32) == target
        peak = jnp.max(logits, axis=1, keepdims=True)
        value = jnp.exp(logits - peak)
        rest = jnp.where(hit, 0.0, value)
        e_all[gz, pair] = rest.astype(BF16)
        for i, (dx, flip) in enumerate(GROUP):
            slot = e_all.at[gz, pair]
            remote(slot, slot, e_ss.at[i], e_rs.at[gz], (z, y, member(dx, flip))).start()
        total = jnp.sum(rest, axis=1, keepdims=True)
        chosen = jnp.sum(jnp.where(hit, value, 0.0), axis=1, keepdims=True)
        lane = lax.broadcasted_iota(I32, (16, 128), 1)
        stat_col[rows, :] = jnp.where(lane == 0, peak, jnp.where(lane == 1, total, jnp.where(lane == 2, chosen, 0.0)))

    for s in range(6):
        if s < 4:
            multiply(s)
        if 1 <= s < 5:
            pass_on(s - 1)
        if s >= 2:
            finish(s - 2)

    def exchange(buf, ss, rs, kind):
        for d in FAR_FIRST:
            c = remote(buf.at[0], buf.at[d], ss.at[d], rs.at[d], along(kind, d))
            c.start()
            sends.append(c)
        for d in FAR_FIRST:
            arrived(buf.at[d], rs.at[d], along(kind, d))
        return combine(buf[...])

    mine = stat_col[...].T[0:8, :]
    st_a[0] = mine
    peak, total, chosen = exchange(st_a, sa_ss, sa_rs, 0)
    st_b[0] = rows_of(peak, total, chosen)
    peak, total, chosen = exchange(st_b, sb_ss, sb_rs, 1)
    used = lax.broadcasted_iota(I32, (1, 128), 1) < 64
    scale = up_row / jnp.where(used, total + chosen, 1.0)
    st_c[gz] = rows_of(scale * jnp.exp(mine[0:1, :] - peak), -scale * total, tgt_row)
    for i, (dx, flip) in enumerate(GROUP):
        c = remote(st_c.at[gz], st_c.at[gz], sc_ss.at[i], sc_rs.at[gz], (z, y, member(dx, flip)))
        c.start()
        sends.append(c)
    for i, (dx, flip) in enumerate(GROUP):
        j = member(dx, flip)
        arrived(e_all.at[j], e_rs.at[j], sibling)
    for i, (dx, flip) in enumerate(GROUP):
        j = member(dx, flip)
        arrived(st_c.at[j], sc_rs.at[j], sibling)
    t_col[...] = jnp.concatenate([st_c[...].reshape(64, 128), jnp.zeros((64, 128), F32)], axis=0).T

    def logit_grads(kind, pair):
        column = (lax.broadcasted_iota(I32, (16, vocab), 1) + (z * 8 + y) * vocab).astype(F32)
        info = t_col[pl.ds(pl.multiple_of(pair * 16, 16), 16), :]
        for x in range(4):
            j = 2 * x + kind
            value = info[:, 8 * j : 8 * j + 1] * e_all[j, pair].astype(F32)
            value = jnp.where(column == info[:, 8 * j + 2 : 8 * j + 3], info[:, 8 * j + 1 : 8 * j + 2], value)
            g[kind, 2 * pair + x // 2, 16 * (x % 2) : 16 * (x % 2) + 16, :] = value.astype(BF16)

    for step, change in enumerate((2, 1, 3, 0)):
        pairs = ((zp + change) % 4, (yp + change) % 4)
        for kind in (0, 1):
            logit_grads(kind, pairs[kind])

        def tile(n, _):
            lanes = pl.ds(pl.multiple_of(n * 256, 256), 256)
            lhs = jnp.concatenate([g[kind, pl.ds(2 * pairs[kind], 2)].reshape(64, vocab) for kind in (0, 1)], axis=0)
            part = lax.dot_general(lhs, w[lanes, :], contract, preferred_element_type=F32).astype(BF16)
            for kind in (0, 1):
                p[kind, pl.ds(2 * pairs[kind], 2), :, lanes] = part[64 * kind : 64 * kind + 64].reshape(2, 32, 256)
            return 0

        lax.fori_loop(0, 4, tile, 0)
        for kind in (0, 1):
            if change == 0:
                chunks = [4 * pairs[kind] + 1 - me[kind]]
                r1[kind, me[kind]] = p[kind, me[kind]]
            else:
                chunks = [2 * pairs[kind], 2 * pairs[kind] + 1]
            for i, q in enumerate(chunks):
                to = (q, y, gz) if kind == 0 else (z, q, gz)
                c = remote(p.at[kind, q], r1.at[kind, me[kind]], d1_ss.at[kind, 2 * step + i], d1_rs.at[kind, me[kind]], to)
                c.start()
                sends.append(c)

    def weight_tile(n, _):
        lanes = pl.ds(pl.multiple_of(n * 256, 256), 256)
        part = lax.dot_general(
            hid[:, :, :, lanes].reshape(512, 256), g[...].reshape(512, vocab), (((0,), (0,)), ((), ())),
            preferred_element_type=F32,
        )
        gwv[lanes, :] = part.astype(BF16)
        return 0

    lax.fori_loop(0, 4, weight_tile, 0)
    store_gw = pltpu.make_async_copy(gwv, gw_hbm, gw_sem)
    store_gw.start()

    for kind in (0, 1):
        for d in range(1, 8):
            src = (me[kind] + d) % 8
            arrived(r1.at[kind, src], d1_rs.at[kind, src], along(1 - kind, 1))
        for b in range(2):
            rows = sum(r1[kind, src, 16 * b : 16 * b + 16, :].astype(F32) for src in range(8))
            for q in range(2):
                low, high = pack(rows[8 * q : 8 * q + 8])
                s2[kind, 4 * b + 2 * q] = low.astype(BF16)
                s2[kind, 4 * b + 2 * q + 1] = high.astype(BF16)
        for d in FAR_FIRST:
            to = (me[1 - kind] + d) % 8
            c = remote(s2.at[kind, to], r2.at[kind, d], d2_ss.at[kind, d], d2_rs.at[kind, d], along(kind, d))
            c.start()
            sends.append(c)
    halves = []
    for kind in (0, 1):
        for d in FAR_FIRST:
            arrived(r2.at[kind, d], d2_rs.at[kind, d], along(kind, 1))
        halves.append(s2[kind, me[1 - kind]].astype(F32) + sum(r2[kind, d].astype(F32) for d in range(1, 8)))
    gh_ref[...] = unpack(*halves).astype(BF16)

    for c in sends:
        c.wait_send()
    for i, (dx, flip) in enumerate(GROUP):
        remote(e_all.at[gz], e_all.at[gz], e_ss.at[i], e_rs.at[gz], sibling).wait_send()
    store_gw.wait()


def body(hidden_states, weight, targets, upstream):
    vmem = pl.BlockSpec(memory_space=pltpu.VMEM)
    hbm = pl.BlockSpec(memory_space=pl.ANY)
    dma = pltpu.SemaphoreType.DMA
    scratch = [
        pltpu.VMEM((1024, 1024), BF16),
        pltpu.VMEM((2, 8, 32, 1024), BF16),
        pltpu.VMEM((2, 16, 256), BF16),
        pltpu.VMEM((2, 8, 16, 256), BF16),
        pltpu.VMEM((4, 64, 1024), F32),
        pltpu.VMEM((4, 64, 1024), F32),
        pltpu.VMEM((4, 64, 1024), F32),
        pltpu.VMEM((4, 64, 1024), F32),
        pltpu.VMEM((4, 3, 16, 1024), F32),
        pltpu.VMEM((8, 4, 16, 1024), BF16),
        pltpu.VMEM((2, 8, 32, 1024), BF16),
        pltpu.VMEM((2, 8, 32, 1024), BF16),
        pltpu.VMEM((2, 8, 32, 1024), BF16),
        pltpu.VMEM((2, 8, 16, 256), BF16),
        pltpu.VMEM((2, 8, 16, 256), BF16),
        pltpu.VMEM((1024, 1024), BF16),
        pltpu.VMEM((128, 128), F32),
        pltpu.VMEM((128, 128), F32),
        pltpu.VMEM((8, 8, 128), F32),
        pltpu.VMEM((8, 8, 128), F32),
        pltpu.VMEM((8, 8, 128), F32),
        pltpu.VMEM((128, 128), F32),
        dma, dma,
        dma((2, 8)), dma((2, 8)), dma((2, 8)), dma((2, 8)),
        dma((4,)), dma((4,)), dma((4, 3)), dma((4, 3)),
        dma((7,)), dma((8,)),
        dma((8,)), dma((8,)), dma((8,)), dma((8,)), dma((7,)), dma((8,)),
        dma((2, 8)), dma((2, 8)), dma((2, 8)), dma((2, 8)),
    ]
    return pl.pallas_call(
        kernel,
        out_shape=(
            jax.ShapeDtypeStruct(hidden_states.shape, BF16),
            jax.ShapeDtypeStruct(weight.shape, BF16),
        ),
        in_specs=[vmem, hbm, vmem, vmem],
        out_specs=(vmem, hbm),
        scratch_shapes=scratch,
        name="projection_backward",
        cost_estimate=pl.CostEstimate(flops=3 * 2 * 512 * 1024 * 1024, bytes_accessed=5 << 20, transcendentals=1 << 16),
        compiler_params=pltpu.CompilerParams(collective_id=0, has_side_effects=True, vmem_limit_bytes=48 << 20),
    )(hidden_states, weight, targets.reshape(1, 512), upstream.reshape(1, 512))


def solution(mesh):
    return jax.shard_map(
        body,
        mesh=mesh,
        in_specs=(P(("gx", "gy"), "gz"), P("gz", ("gx", "gy")), P(), P()),
        out_specs=(P(("gx", "gy"), "gz"), P("gz", ("gx", "gy"))),
        check_vma=False,
    )
```

```python
import functools

import jax
import jax.numpy as jnp
from jax import lax
from jax.experimental import pallas as pl
from jax.experimental.pallas import tpu as pltpu
from jax.sharding import PartitionSpec as P

MESH = pl.DeviceIdType.MESH
F32, BF16, I32 = jnp.float32, jnp.bfloat16, jnp.int32
FAR_FIRST = (4, 3, 5, 2, 6, 1, 7)
GROUP = ((2, 0), (2, 1), (1, 0), (3, 0), (1, 1), (3, 1), (0, 1))


def remote(src, dst, send_sem, recv_sem, device):
    return pltpu.make_async_remote_copy(
        src_ref=src, dst_ref=dst, send_sem=send_sem, recv_sem=recv_sem, device_id=device, device_id_type=MESH
    )


def upper_rows(shape):
    return lax.broadcasted_iota(I32, shape, 0) < 4


def pack(a):
    q = [a[:, 256 * k : 256 * (k + 1)] for k in range(4)]
    t = [pltpu.roll(x, 4, 0) for x in q]
    first = upper_rows((8, 256))
    low = jnp.concatenate([jnp.where(first, q[0], t[1]), jnp.where(first, q[2], t[3])], axis=0)
    high = jnp.concatenate([jnp.where(first, t[0], q[1]), jnp.where(first, t[2], q[3])], axis=0)
    return low, high


def unpack(low, high):
    first = upper_rows((8, 256))
    parts = []
    for k in range(2):
        a, c = low[8 * k : 8 * k + 8], high[8 * k : 8 * k + 8]
        parts.append(jnp.where(first, a, pltpu.roll(c, 4, 0)))
        parts.append(jnp.where(first, pltpu.roll(a, 4, 0), c))
    return jnp.concatenate(parts, axis=1)


def rows_of(*rows):
    sub = lax.broadcasted_iota(I32, (8, 128), 0)
    out = jnp.zeros((8, 128), F32)
    for k, row in enumerate(rows):
        out = jnp.where(sub == k, jnp.broadcast_to(row, (8, 128)), out)
    return out


def combine(stats):
    peaks = [stats[k, 0:1, :] for k in range(stats.shape[0])]
    peak = functools.reduce(jnp.maximum, peaks)
    scale = [jnp.exp(p - peak) for p in peaks]
    total = sum(stats[k, 1:2, :] * scale[k] for k in range(stats.shape[0]))
    chosen = sum(stats[k, 2:3, :] * scale[k] for k in range(stats.shape[0]))
    return peak, total, chosen


def kernel(
    h_hbm, w_hbm, tgt_hbm, up_hbm, gh_ref, gw_ref,
    w, wt, h_ref, tgt_ref, up_ref, hid, a1s, a1r, keep, cs, cr, xs, xr, e_all, g, p, r1, s2, r2,
    own_col, stat_col, st_a, st_b, st_c, t_col,
    w_sem, in_sem, a1_ss, a1_rs, a2_ss, a2_rs, c_ss, c_rs, x_ss, x_rs,
    e_ss, e_rs, sa_ss, sa_rs, sb_ss, sb_rs, sc_ss, sc_rs, d1_ss, d1_rs, d2_ss, d2_rs,
):
    z, y, gz = lax.axis_index("gx"), lax.axis_index("gy"), lax.axis_index("gz")
    xx, core = gz // 2, gz % 2
    vocab = w.shape[1]
    zp, yp = z // 2, y // 2
    me = (z, y)

    def along(kind, d):
        return (z, (y + d) % 8, gz) if kind == 0 else ((z + d) % 8, y, gz)

    def member(dx, flip):
        c = 1 - core if flip else core
        return ((xx + dx) % 4) * 2 + c

    load_w = pltpu.make_async_copy(w_hbm, w, w_sem)
    load_w.start()
    loads = [
        pltpu.make_async_copy(src, dst, in_sem.at[i])
        for i, (src, dst) in enumerate(((h_hbm, h_ref), (tgt_hbm, tgt_ref), (up_hbm, up_ref)))
    ]
    for c in loads:
        c.start()

    barrier = pltpu.get_barrier_semaphore()
    for d in FAR_FIRST:
        for kind in (0, 1):
            pl.semaphore_signal(barrier, inc=1, device_id=along(kind, d), device_id_type=MESH)
    for dx, flip in GROUP:
        pl.semaphore_signal(barrier, inc=1, device_id=(z, y, member(dx, flip)), device_id_type=MESH)

    for c in loads:
        c.wait()
    low, high = pack(h_ref[...].astype(F32))
    a1s[0] = low.astype(BF16)
    a1s[1] = high.astype(BF16)
    a1r[0, y] = low.astype(BF16)
    a1r[1, z] = high.astype(BF16)

    k = lax.broadcasted_iota(I32, (128, 512), 0)
    t = lax.broadcasted_iota(I32, (128, 512), 1)
    block = 2 * (k >> 4) + xx // 2
    other = (xx % 2) * 4 + ((k >> 2) & 3)
    zt = jnp.where(core == 0, block, other)
    yt = jnp.where(core == 0, other, block)
    token = zt * 64 + yt * 8 + core * 4 + (k & 3)
    select = jnp.where((token == t) & (k < 64), 1.0, 0.0).astype(BF16)
    tgt = tgt_ref[...]
    sub = lax.broadcasted_iota(I32, (128, 512), 0)
    values = jnp.where(sub == 0, jnp.broadcast_to((tgt >> 8).astype(F32), (128, 512)), 0.0)
    values = jnp.where(sub == 1, jnp.broadcast_to((tgt & 255).astype(F32), (128, 512)), values)
    values = jnp.where(sub == 2, jnp.broadcast_to(up_ref[...].reshape(1, 512).astype(F32), (128, 512)), values).astype(BF16)
    contract = (((1,), (1,)), ((), ()))
    own_col[...] = lax.dot_general(select, values, contract, preferred_element_type=F32)
    own_row = lax.dot_general(values, select, contract, preferred_element_type=F32)
    tgt_row = own_row[0:1, :] * 256.0 + own_row[1:2, :]
    up_row = own_row[2:3, :]
    stat_col[...] = jnp.zeros((128, 128), F32)
    load_w.wait()

    def turn(n, _):
        lanes = pl.ds(pl.multiple_of(n * 256, 256), 256)
        wt[:, lanes] = w[lanes, :].T
        return 0

    lax.fori_loop(0, 4, turn, 0)

    pl.semaphore_wait(barrier, 21)

    sends = []
    for d in FAR_FIRST:
        for kind in (0, 1):
            c = remote(a1s.at[kind], a1r.at[kind, me[1 - kind]], a1_ss.at[kind, d], a1_rs.at[kind, me[1 - kind]], along(kind, d))
            c.start()
            sends.append(c)

    def arrived(dst, sem, peer):
        remote(dst, dst, sem, sem, peer).wait_recv()

    for kind in (0, 1):
        mine = me[1 - kind]
        for d in range(1, 8):
            src = (mine + d) % 8
            arrived(a1r.at[kind, src], a1_rs.at[kind, src], along(kind, 1))
        for b in range(2):
            rows = [
                unpack(a1r[kind, 4 * b + 2 * q].astype(F32), a1r[kind, 4 * b + 2 * q + 1].astype(F32)) for q in range(2)
            ]
            hid[kind, me[kind], 16 * b : 16 * b + 16, :] = jnp.concatenate(rows, axis=0).astype(BF16)
        for d in (1, 7, 2, 6, 3, 5, 4):
            slot = hid.at[kind, me[kind]]
            c = remote(slot, slot, a2_ss.at[kind, d], a2_rs.at[kind, me[kind]], along(1 - kind, d))
            c.start()
            sends.append(c)

    def shift(s, parity):
        return (0, 2 * parity + 3, 5 - 2 * parity, 2)[s]

    def pair_of(kind, s):
        return (zp + shift(s, z % 2)) % 4 if kind == 0 else (yp + shift(s, y % 2)) % 4

    def own_pair(s):
        return jnp.where(core == 0, pair_of(0, s), pair_of(1, s))

    def other_pair(s):
        return jnp.where(core == 0, pair_of(1, s), pair_of(0, s))

    sibling = (z, y, member(0, 1))

    def multiply(s):
        for kind in (0, 1):
            pair = pair_of(kind, s)
            if s == 0:
                chunks = [4 * pair + 1 - me[kind]]
            else:
                chunks = [2 * pair, 2 * pair + 1]
            for q in chunks:
                arrived(hid.at[kind, q], a2_rs.at[kind, q], along(1 - kind, 1))
        mine, others = own_pair(s), other_pair(s)

        lhs = jnp.concatenate(
            [hid[core, pl.ds(2 * mine, 2)].reshape(64, 1024), hid[1 - core, pl.ds(2 * others, 2)].reshape(64, 1024)], axis=0
        )
        part = jnp.dot(lhs, w[...], preferred_element_type=F32)
        cs[s] = part[64:]
        keep[s] = part[:64]
        c = remote(cs.at[s], cr.at[s], c_ss.at[s], c_rs.at[s], sibling)
        c.start()
        sends.append(c)

    def pass_on(s):
        arrived(cr.at[s], c_rs.at[s], sibling)
        xs[s] = keep[s] + cr[s]
        for dx in (2, 1, 3):
            to = (xx + dx) % 4
            c = remote(
                xs.at[s, pl.ds(pl.multiple_of(to * 16, 16), 16)], xr.at[s, dx - 1], x_ss.at[s, dx - 1], x_rs.at[s, dx - 1],
                (z, y, member(dx, 0)),
            )
            c.start()
            sends.append(c)

    def finish(s):
        for dx in (2, 1, 3):
            arrived(xr.at[s, dx - 1], x_rs.at[s, dx - 1], sibling)
        pair = own_pair(s)
        logits = xs[s, pl.ds(pl.multiple_of(xx * 16, 16), 16), :] + xr[s, 0] + xr[s, 1] + xr[s, 2]
        rows = pl.ds(pl.multiple_of(pair * 16, 16), 16)
        info = own_col[rows, :]
        target = info[:, 0:1] * 256.0 + info[:, 1:2]
        column = lax.broadcasted_iota(I32, (16, vocab), 1) + (z * 8 + y) * vocab
        hit = column.astype(F32) == target
        peak = jnp.max(logits, axis=1, keepdims=True)
        value = jnp.exp(logits - peak)
        rest = jnp.where(hit, 0.0, value)
        e_all[gz, pair] = rest.astype(BF16)
        total = jnp.sum(rest, axis=1, keepdims=True)
        chosen = jnp.sum(jnp.where(hit, value, 0.0), axis=1, keepdims=True)
        lane = lax.broadcasted_iota(I32, (16, 128), 1)
        stat_col[rows, :] = jnp.where(lane == 0, peak, jnp.where(lane == 1, total, jnp.where(lane == 2, chosen, 0.0)))

    for s in range(4):
        multiply(s)
        pass_on(s)
        if s >= 2:
            finish(s - 2)
    finish(2)
    finish(3)

    def give(buf, ss, rs, kind):
        for d in FAR_FIRST:
            c = remote(buf.at[0], buf.at[d], ss.at[d], rs.at[d], along(kind, d))
            c.start()
            sends.append(c)

    def take(buf, rs, kind):
        for d in FAR_FIRST:
            arrived(buf.at[d], rs.at[d], along(kind, d))
        return combine(buf[...])

    def share(j, i, to):
        c = remote(e_all.at[j], e_all.at[j], e_ss.at[i], e_rs.at[j], (z, y, to))
        c.start()
        sends.append(c)

    mine = stat_col[...].T[0:8, :]
    st_a[0] = mine
    give(st_a, sa_ss, sa_rs, 0)
    for dx in (2, 1, 3):
        share(gz, dx, member(dx, 0))
    share(gz, 0, member(0, 1))
    peak, total, chosen = take(st_a, sa_rs, 0)
    st_b[0] = rows_of(peak, total, chosen)
    give(st_b, sb_ss, sb_rs, 1)
    for dx in (1, 3, 2):
        j = member(dx, 0)
        arrived(e_all.at[j], e_rs.at[j], sibling)
        share(j, 3 + dx, member(0, 1))
    peak, total, chosen = take(st_b, sb_rs, 1)
    used = lax.broadcasted_iota(I32, (1, 128), 1) < 64
    scale = up_row / jnp.where(used, total + chosen, 1.0)
    st_c[gz] = rows_of(scale * jnp.exp(mine[0:1, :] - peak), -scale * total, tgt_row)
    for i, (dx, flip) in enumerate(GROUP):
        c = remote(st_c.at[gz], st_c.at[gz], sc_ss.at[i], sc_rs.at[gz], (z, y, member(dx, flip)))
        c.start()
        sends.append(c)
    for dx in range(4):
        j = member(dx, 1)
        arrived(e_all.at[j], e_rs.at[j], sibling)
    for i, (dx, flip) in enumerate(GROUP):
        j = member(dx, flip)
        arrived(st_c.at[j], sc_rs.at[j], sibling)
    t_col[...] = jnp.concatenate([st_c[...].reshape(64, 128), jnp.zeros((64, 128), F32)], axis=0).T

    def logit_grads(kind, pair):
        column = (lax.broadcasted_iota(I32, (16, vocab), 1) + (z * 8 + y) * vocab).astype(F32)
        info = t_col[pl.ds(pl.multiple_of(pair * 16, 16), 16), :]
        for x in range(4):
            j = 2 * x + kind
            value = info[:, 8 * j : 8 * j + 1] * e_all[j, pair].astype(F32)
            value = jnp.where(column == info[:, 8 * j + 2 : 8 * j + 3], info[:, 8 * j + 1 : 8 * j + 2], value)
            g[kind, 2 * pair + x // 2, 16 * (x % 2) : 16 * (x % 2) + 16, :] = value.astype(BF16)

    for step, change in enumerate((2, 1, 3, 0)):
        pairs = ((zp + change) % 4, (yp + change) % 4)
        for kind in (0, 1):
            logit_grads(kind, pairs[kind])

        lhs = jnp.concatenate([g[kind, pl.ds(2 * pairs[kind], 2)].reshape(64, vocab) for kind in (0, 1)], axis=0)
        part = jnp.dot(lhs, wt[...], preferred_element_type=F32).astype(BF16)
        for kind in (0, 1):
            p[kind, pl.ds(2 * pairs[kind], 2)] = part[64 * kind : 64 * kind + 64].reshape(2, 32, 1024)
        for kind in (0, 1):
            if change == 0:
                chunks = [4 * pairs[kind] + 1 - me[kind]]
                r1[kind, me[kind]] = p[kind, me[kind]]
            else:
                chunks = [2 * pairs[kind], 2 * pairs[kind] + 1]
            for i, q in enumerate(chunks):
                to = (q, y, gz) if kind == 0 else (z, q, gz)
                c = remote(p.at[kind, q], r1.at[kind, me[kind]], d1_ss.at[kind, 2 * step + i], d1_rs.at[kind, me[kind]], to)
                c.start()
                sends.append(c)

    def weight_tile(n, _):
        lanes = pl.ds(pl.multiple_of(n * 256, 256), 256)
        part = lax.dot_general(
            hid[:, :, :, lanes].reshape(512, 256), g[...].reshape(512, vocab), (((0,), (0,)), ((), ())),
            preferred_element_type=F32,
        )
        gw_ref[lanes, :] = part.astype(BF16)
        return 0

    lax.fori_loop(0, 4, weight_tile, 0)

    for kind in (0, 1):
        for d in range(1, 8):
            src = (me[kind] + d) % 8
            arrived(r1.at[kind, src], d1_rs.at[kind, src], along(1 - kind, 1))
        for b in range(2):
            rows = sum(r1[kind, src, 16 * b : 16 * b + 16, :].astype(F32) for src in range(8))
            for q in range(2):
                low, high = pack(rows[8 * q : 8 * q + 8])
                s2[kind, 4 * b + 2 * q] = low.astype(BF16)
                s2[kind, 4 * b + 2 * q + 1] = high.astype(BF16)
        for d in FAR_FIRST:
            to = (me[1 - kind] + d) % 8
            c = remote(s2.at[kind, to], r2.at[kind, d], d2_ss.at[kind, d], d2_rs.at[kind, d], along(kind, d))
            c.start()
            sends.append(c)
    halves = []
    for kind in (0, 1):
        for d in FAR_FIRST:
            arrived(r2.at[kind, d], d2_rs.at[kind, d], along(kind, 1))
        halves.append(s2[kind, me[1 - kind]].astype(F32) + sum(r2[kind, d].astype(F32) for d in range(1, 8)))
    gh_ref[...] = unpack(*halves).astype(BF16)

    for c in sends:
        c.wait_send()


def body(hidden_states, weight, targets, upstream):
    vmem = pl.BlockSpec(memory_space=pltpu.VMEM)
    hbm = pl.BlockSpec(memory_space=pltpu.HBM)
    dma = pltpu.SemaphoreType.DMA
    scratch = [
        pltpu.VMEM((1024, 1024), BF16),
        pltpu.VMEM((1024, 1024), BF16),
        pltpu.VMEM((8, 1024), BF16),
        pltpu.VMEM((1, 512), I32),
        pltpu.VMEM((512,), BF16),
        pltpu.VMEM((2, 8, 32, 1024), BF16),
        pltpu.VMEM((2, 16, 256), BF16),
        pltpu.VMEM((2, 8, 16, 256), BF16),
        pltpu.VMEM((4, 64, 1024), F32),
        pltpu.VMEM((4, 64, 1024), F32),
        pltpu.VMEM((4, 64, 1024), F32),
        pltpu.VMEM((4, 64, 1024), F32),
        pltpu.VMEM((4, 3, 16, 1024), F32),
        pltpu.VMEM((8, 4, 16, 1024), BF16),
        pltpu.VMEM((2, 8, 32, 1024), BF16),
        pltpu.VMEM((2, 8, 32, 1024), BF16),
        pltpu.VMEM((2, 8, 32, 1024), BF16),
        pltpu.VMEM((2, 8, 16, 256), BF16),
        pltpu.VMEM((2, 8, 16, 256), BF16),
        pltpu.VMEM((128, 128), F32),
        pltpu.VMEM((128, 128), F32),
        pltpu.VMEM((8, 8, 128), F32),
        pltpu.VMEM((8, 8, 128), F32),
        pltpu.VMEM((8, 8, 128), F32),
        pltpu.VMEM((128, 128), F32),
        dma, dma((3,)),
        dma((2, 8)), dma((2, 8)), dma((2, 8)), dma((2, 8)),
        dma((4,)), dma((4,)), dma((4, 3)), dma((4, 3)),
        dma((7,)), dma((8,)),
        dma((8,)), dma((8,)), dma((8,)), dma((8,)), dma((7,)), dma((8,)),
        dma((2, 8)), dma((2, 8)), dma((2, 8)), dma((2, 8)),
    ]
    operands = [
        pltpu.with_memory_space_constraint(a, pltpu.HBM)
        for a in (hidden_states, weight, targets.reshape(1, 512), upstream)
    ]
    return pl.pallas_call(
        kernel,
        out_shape=(
            jax.ShapeDtypeStruct(hidden_states.shape, BF16),
            jax.ShapeDtypeStruct(weight.shape, BF16),
        ),
        in_specs=[hbm, hbm, hbm, hbm],
        out_specs=(vmem, vmem),
        scratch_shapes=scratch,
        name="projection_backward",
        cost_estimate=pl.CostEstimate(flops=3 * 2 * 512 * 1024 * 1024, bytes_accessed=5 << 20, transcendentals=1 << 16),
        compiler_params=pltpu.CompilerParams(collective_id=0, has_side_effects=True, vmem_limit_bytes=48 << 20),
    )(*operands)


def solution(mesh):
    return jax.shard_map(
        body,
        mesh=mesh,
        in_specs=(P(("gx", "gy"), "gz"), P("gz", ("gx", "gy")), P(), P()),
        out_specs=(P(("gx", "gy"), "gz"), P("gz", ("gx", "gy"))),
        check_vma=False,
    )
```

```python
import functools

import jax
import jax.numpy as jnp
from jax import lax
from jax.experimental import pallas as pl
from jax.experimental.pallas import tpu as pltpu
from jax.sharding import PartitionSpec as P

MESH = pl.DeviceIdType.MESH
F32, BF16, I32 = jnp.float32, jnp.bfloat16, jnp.int32
FAR_FIRST = (4, 3, 5, 2, 6, 1, 7)
GROUP = ((2, 0), (2, 1), (1, 0), (3, 0), (1, 1), (3, 1), (0, 1))


def remote(src, dst, send_sem, recv_sem, device):
    return pltpu.make_async_remote_copy(
        src_ref=src, dst_ref=dst, send_sem=send_sem, recv_sem=recv_sem, device_id=device, device_id_type=MESH
    )


def upper_rows(shape):
    return lax.broadcasted_iota(I32, shape, 0) < 4


def pack(a):
    q = [a[:, 256 * k : 256 * (k + 1)] for k in range(4)]
    t = [pltpu.roll(x, 4, 0) for x in q]
    first = upper_rows((8, 256))
    low = jnp.concatenate([jnp.where(first, q[0], t[1]), jnp.where(first, q[2], t[3])], axis=0)
    high = jnp.concatenate([jnp.where(first, t[0], q[1]), jnp.where(first, t[2], q[3])], axis=0)
    return low, high


def unpack(low, high):
    first = upper_rows((8, 256))
    parts = []
    for k in range(2):
        a, c = low[8 * k : 8 * k + 8], high[8 * k : 8 * k + 8]
        parts.append(jnp.where(first, a, pltpu.roll(c, 4, 0)))
        parts.append(jnp.where(first, pltpu.roll(a, 4, 0), c))
    return jnp.concatenate(parts, axis=1)


def rows_of(*rows):
    sub = lax.broadcasted_iota(I32, (8, 128), 0)
    out = jnp.zeros((8, 128), F32)
    for k, row in enumerate(rows):
        out = jnp.where(sub == k, jnp.broadcast_to(row, (8, 128)), out)
    return out


def combine(stats):
    peaks = [stats[k, 0:1, :] for k in range(stats.shape[0])]
    peak = functools.reduce(jnp.maximum, peaks)
    scale = [jnp.exp(p - peak) for p in peaks]
    total = sum(stats[k, 1:2, :] * scale[k] for k in range(stats.shape[0]))
    chosen = sum(stats[k, 2:3, :] * scale[k] for k in range(stats.shape[0]))
    return peak, total, chosen


def kernel(
    h_hbm, w_hbm, tgt_hbm, up_hbm, gh_ref, gw_ref,
    w, wt, h_ref, tgt_ref, up_ref, hid, a1s, a1r, keep, cs, cr, xs, xr, e_all, g, p, r1, s2, r2,
    tp, tr, tg, th, own_col, all_col, stat_col, st_a, st_b, st_c, t_col, d_col,
    w_sem, in_sem, a1_ss, a1_rs, a2_ss, a2_rs, a2_hs, c_ss, c_rs, x_ss, x_rs,
    e_ss, e_rs, sa_ss, sa_rs, sb_ss, sb_rs, sc_ss, sc_rs, t_ss, t_rs, d1_ss, d1_rs, d2_ss, d2_rs,
):
    z, y, gz = lax.axis_index("gx"), lax.axis_index("gy"), lax.axis_index("gz")
    xx, core = gz // 2, gz % 2
    vocab = w.shape[1]
    zp, yp = z // 2, y // 2
    first_column = (z * 8 + y) * vocab
    contract = (((1,), (1,)), ((), ()))
    me = (z, y)

    def along(kind, d):
        return (z, (y + d) % 8, gz) if kind == 0 else ((z + d) % 8, y, gz)

    def member(dx, flip):
        c = 1 - core if flip else core
        return ((xx + dx) % 4) * 2 + c

    load_w = pltpu.make_async_copy(w_hbm, w, w_sem)
    load_w.start()
    loads = [
        pltpu.make_async_copy(src, dst, in_sem.at[i])
        for i, (src, dst) in enumerate(((h_hbm, h_ref), (tgt_hbm, tgt_ref), (up_hbm, up_ref)))
    ]
    for c in loads:
        c.start()

    barrier = pltpu.get_barrier_semaphore()
    for d in FAR_FIRST:
        for kind in (0, 1):
            pl.semaphore_signal(barrier, inc=1, device_id=along(kind, d), device_id_type=MESH)
    for dx, flip in GROUP:
        pl.semaphore_signal(barrier, inc=1, device_id=(z, y, member(dx, flip)), device_id_type=MESH)

    for c in loads:
        c.wait()
    low, high = pack(h_ref[...].astype(F32))
    a1s[0] = low.astype(BF16)
    a1s[1] = high.astype(BF16)
    a1r[0, y] = low.astype(BF16)
    a1r[1, z] = high.astype(BF16)

    pl.semaphore_wait(barrier, 21)

    sends = []
    for d in FAR_FIRST:
        for kind in (0, 1):
            c = remote(a1s.at[kind], a1r.at[kind, me[1 - kind]], a1_ss.at[kind, d], a1_rs.at[kind, me[1 - kind]], along(kind, d))
            c.start()
            sends.append(c)

    def arrived(dst, sem, peer):
        remote(dst, dst, sem, sem, peer).wait_recv()

    k = lax.broadcasted_iota(I32, (128, 512), 0)
    t = lax.broadcasted_iota(I32, (128, 512), 1)
    block = 2 * (k >> 4) + xx // 2
    other = (xx % 2) * 4 + ((k >> 2) & 3)
    zt = jnp.where(core == 0, block, other)
    yt = jnp.where(core == 0, other, block)
    token = zt * 64 + yt * 8 + core * 4 + (k & 3)
    select = jnp.where((token == t) & (k < 64), 1.0, 0.0).astype(BF16)
    tgt = tgt_ref[...]
    sub = lax.broadcasted_iota(I32, (128, 512), 0)
    values = jnp.where(sub == 0, jnp.broadcast_to((tgt >> 8).astype(F32), (128, 512)), 0.0)
    values = jnp.where(sub == 1, jnp.broadcast_to((tgt & 255).astype(F32), (128, 512)), values)
    values = jnp.where(sub == 2, jnp.broadcast_to(up_ref[...].reshape(1, 512).astype(F32), (128, 512)), values).astype(BF16)
    own_col[...] = lax.dot_general(select, values, contract, preferred_element_type=F32)
    own_row = lax.dot_general(values, select, contract, preferred_element_type=F32)
    tgt_row = own_row[0:1, :] * 256.0 + own_row[1:2, :]
    up_row = own_row[2:3, :]
    stat_col[...] = jnp.zeros((128, 128), F32)
    row = lax.broadcasted_iota(I32, (512, 128), 0)
    first, second = (row >> 5) & 7, (row & 31) >> 2
    token = jnp.where(row < 256, first * 64 + second * 8, second * 64 + first * 8 + 4) + (row & 3)
    order = (token[:, 0:1] == lax.broadcasted_iota(I32, (512, 512), 1)).astype(F32).astype(BF16)
    all_col[...] = lax.dot_general(order, values, contract, preferred_element_type=F32)
    load_w.wait()

    def turn(n, _):
        lanes = pl.ds(pl.multiple_of(n * 256, 256), 256)
        wt[:, lanes] = w[lanes, :].T
        return 0

    lax.fori_loop(0, 4, turn, 0)

    def chosen_rows(b, _):
        info = all_col[pl.ds(pl.multiple_of(b * 128, 128), 128), :]
        target = info[:, 0:1] * 256.0 + info[:, 1:2]
        hit = ((lax.broadcasted_iota(I32, (128, vocab), 1) + first_column).astype(F32) == target).astype(F32)
        part = jnp.dot(hit.astype(BF16), wt[...], preferred_element_type=F32).astype(BF16)
        tp[b // 2, pl.ds((b % 2) * 4, 4)] = part.reshape(4, 32, 1024)
        return 0

    lax.fori_loop(0, 4, chosen_rows, 0)

    def send_chosen(kind, src, dst, i, d):
        c = remote(src, dst, t_ss.at[kind, i], t_rs.at[kind, i], along(1 - kind, d))
        c.start()
        sends.append(c)

    for kind in (0, 1):
        for h, d in enumerate((1, 7)):
            half = pl.ds(16 * h, 16)
            send_chosen(kind, tp.at[kind, (me[kind] + 4) % 8, half], th.at[kind, h], 4 + h, 2 * d)
            send_chosen(kind, tp.at[kind, (me[kind] + 3 * d) % 8], tg.at[kind, h], 2 + h, d)
            send_chosen(kind, tp.at[kind, (me[kind] + d) % 8], tr.at[kind, h], h, d)

    def join_chosen():
        for kind in (0, 1):
            for h, d in enumerate((1, 7)):
                arrived(tg.at[kind, h], t_rs.at[kind, 2 + h], along(1 - kind, 1))
                arrived(th.at[kind, h], t_rs.at[kind, 4 + h], along(1 - kind, 1))
                q = (me[kind] + 2 * d) % 8
                for b in (0, 1):
                    rows = pl.ds(16 * b, 16)
                    total = tp[kind, q, rows, :].astype(F32) + tg[kind, h, rows, :].astype(F32)
                    if b == h:
                        total = total + th[kind, h].astype(F32)
                    tp[kind, q, rows, :] = total.astype(BF16)
                send_chosen(kind, tp.at[kind, q], tr.at[kind, 2 + h], 6 + h, 2 * d)

    for kind in (0, 1):
        mine = me[1 - kind]
        for d in range(1, 8):
            src = (mine + d) % 8
            arrived(a1r.at[kind, src], a1_rs.at[kind, src], along(kind, 1))
        for b in range(2):
            rows = [
                unpack(a1r[kind, 4 * b + 2 * q].astype(F32), a1r[kind, 4 * b + 2 * q + 1].astype(F32)) for q in range(2)
            ]
            hid[kind, me[kind], 16 * b : 16 * b + 16, :] = jnp.concatenate(rows, axis=0).astype(BF16)
        for d in (2, 6, 1, 7):
            slot = hid.at[kind, me[kind]]
            c = remote(slot, slot, a2_ss.at[kind, d], a2_rs.at[kind, me[kind]], along(1 - kind, d))
            c.start()
            sends.append(c)

    def shift(s, parity):
        return (0, 2 * parity + 3, 5 - 2 * parity, 2)[s]

    def pair_of(kind, s):
        return (zp + shift(s, z % 2)) % 4 if kind == 0 else (yp + shift(s, y % 2)) % 4

    def own_pair(s):
        return jnp.where(core == 0, pair_of(0, s), pair_of(1, s))

    def other_pair(s):
        return jnp.where(core == 0, pair_of(1, s), pair_of(0, s))

    sibling = (z, y, member(0, 1))

    def relay():
        for kind in (0, 1):
            for h, d in enumerate((1, 7)):
                q = (me[kind] - 2 * d) % 8
                slot = hid.at[kind, q]
                arrived(slot, a2_rs.at[kind, q], along(1 - kind, 1))
                c = remote(slot, slot, a2_ss.at[kind, 3 + 2 * h], a2_rs.at[kind, q], along(1 - kind, d))
                c.start()
                sends.append(c)
                half = hid.at[kind, q, 16 * h : 16 * h + 16]
                c = remote(half, half, a2_ss.at[kind, 4 * h], a2_hs.at[kind, h], along(1 - kind, 2 * d))
                c.start()
                sends.append(c)

    def multiply(s):
        for kind in (0, 1):
            q = 2 * pair_of(kind, s) + 1 - me[kind] % 2
            arrived(hid.at[kind, q], a2_rs.at[kind, q], along(1 - kind, 1))
            if s == 3:
                q = (me[kind] + 4) % 8
                for h in (0, 1):
                    arrived(hid.at[kind, q, 16 * h : 16 * h + 16], a2_hs.at[kind, h], along(1 - kind, 1))
        mine, others = own_pair(s), other_pair(s)

        lhs = jnp.concatenate(
            [hid[core, pl.ds(2 * mine, 2)].reshape(64, 1024), hid[1 - core, pl.ds(2 * others, 2)].reshape(64, 1024)], axis=0
        )
        part = jnp.dot(lhs, w[...], preferred_element_type=F32)
        cs[s] = part[64:]
        keep[s] = part[:64]
        c = remote(cs.at[s], cr.at[s], c_ss.at[s], c_rs.at[s], sibling)
        c.start()
        sends.append(c)

    def pass_on(s):
        arrived(cr.at[s], c_rs.at[s], sibling)
        xs[s] = keep[s] + cr[s]
        for dx in (2, 1, 3):
            to = (xx + dx) % 4
            c = remote(
                xs.at[s, pl.ds(pl.multiple_of(to * 16, 16), 16)], xr.at[s, dx - 1], x_ss.at[s, dx - 1], x_rs.at[s, dx - 1],
                (z, y, member(dx, 0)),
            )
            c.start()
            sends.append(c)

    def finish(s):
        for dx in (2, 1, 3):
            arrived(xr.at[s, dx - 1], x_rs.at[s, dx - 1], sibling)
        pair = own_pair(s)
        logits = xs[s, pl.ds(pl.multiple_of(xx * 16, 16), 16), :] + xr[s, 0] + xr[s, 1] + xr[s, 2]
        rows = pl.ds(pl.multiple_of(pair * 16, 16), 16)
        info = own_col[rows, :]
        target = info[:, 0:1] * 256.0 + info[:, 1:2]
        column = lax.broadcasted_iota(I32, (16, vocab), 1) + first_column
        hit = column.astype(F32) == target
        peak = jnp.max(logits, axis=1, keepdims=True)
        value = jnp.exp(logits - peak)
        rest = jnp.where(hit, 0.0, value)
        e_all[gz, pair] = rest.astype(BF16)
        for dx in (2, 1, 3):
            share(gz, pair, s, dx, member(dx, 0))
        share(gz, pair, s, 0, member(0, 1))
        total = jnp.sum(rest, axis=1, keepdims=True)
        chosen = jnp.sum(jnp.where(hit, value, 0.0), axis=1, keepdims=True)
        lane = lax.broadcasted_iota(I32, (16, 128), 1)
        stat_col[rows, :] = jnp.where(lane == 0, peak, jnp.where(lane == 1, total, jnp.where(lane == 2, chosen, 0.0)))

    def share(j, pair, s, i, to):
        slot = e_all.at[j, pair]
        c = remote(slot, slot, e_ss.at[i, s], e_rs.at[j, pair], (z, y, to))
        c.start()
        sends.append(c)

    def forward(s):
        for dx in (1, 3, 2):
            j, pair = member(dx, 0), own_pair(s)
            arrived(e_all.at[j, pair], e_rs.at[j, pair], sibling)
            share(j, pair, s, 3 + dx, member(0, 1))

    def scatter(kind, s):
        pair = pair_of(kind, s)
        if s == 0:
            chunks = [4 * pair + 1 - me[kind]]
            r1[kind, me[kind]] = p[kind, me[kind]]
        else:
            chunks = [2 * pair, 2 * pair + 1]
        for i, q in enumerate(chunks):
            to = (q, y, gz) if kind == 0 else (z, q, gz)
            c = remote(
                p.at[kind, q], r1.at[kind, me[kind]], d1_ss.at[kind, 2 * s + i], d1_rs.at[kind, me[kind]], to
            )
            c.start()
            sends.append(c)

    def terms(s):
        pairs = (pair_of(0, s), pair_of(1, s))
        for dx in range(4):
            j, pair = member(dx, 1), other_pair(s)
            arrived(e_all.at[j, pair], e_rs.at[j, pair], sibling)
        lhs = jnp.concatenate([e_all[2 * x + kind, pairs[kind]] for kind in (0, 1) for x in range(4)], axis=0)
        part = jnp.dot(lhs, wt[...], preferred_element_type=F32).astype(BF16)
        for kind in (0, 1):
            p[kind, pl.ds(2 * pairs[kind], 2)] = part[64 * kind : 64 * kind + 64].reshape(2, 32, 1024)
            scatter(kind, s)

    def stat_peer(phase, d):
        over_z = core == phase
        return (jnp.where(over_z, (z + d) % 8, z), jnp.where(over_z, y, (y + d) % 8), gz)

    def give(buf, ss, rs, phase):
        for d in FAR_FIRST:
            c = remote(buf.at[0], buf.at[d], ss.at[d], rs.at[d], stat_peer(phase, d))
            c.start()
            sends.append(c)

    def take(buf, rs, phase):
        for d in FAR_FIRST:
            arrived(buf.at[d], rs.at[d], stat_peer(phase, d))
        return combine(buf[...])

    def stats_first():
        st_a[0] = stat_col[...].T[0:8, :]
        give(st_a, sa_ss, sa_rs, 0)

    def stats_second():
        st_b[0] = rows_of(*take(st_a, sa_rs, 0))
        give(st_b, sb_ss, sb_rs, 1)

    def stats_third():
        peak, total, chosen = take(st_b, sb_rs, 1)
        used = lax.broadcasted_iota(I32, (1, 128), 1) < 64
        scale = up_row / jnp.where(used, total + chosen, 1.0)
        factors = [scale * jnp.exp(st_a[d, 0:1, :] - peak) for d in range(8)]
        st_c[gz, 0:8] = rows_of(factors[0], -scale * total, tgt_row)
        st_c[gz, 8:16] = rows_of(*factors)
        for i, (dx, flip) in enumerate(GROUP):
            c = remote(st_c.at[gz], st_c.at[gz], sc_ss.at[i], sc_rs.at[gz], (z, y, member(dx, flip)))
            c.start()
            sends.append(c)

    multiply(0)
    relay()
    pass_on(0)
    multiply(1)
    pass_on(1)
    multiply(2)
    finish(0)
    pass_on(2)
    finish(1)
    multiply(3)
    join_chosen()
    forward(0)
    pass_on(3)
    finish(2)
    terms(0)
    forward(1)
    terms(1)
    finish(3)
    stats_first()
    forward(2)
    terms(2)
    forward(3)
    stats_second()
    terms(3)

    for kind in (0, 1):
        for i in (0, 1, 2, 3):
            arrived(tr.at[kind, i], t_rs.at[kind, (0, 1, 6, 7)[i]], along(1 - kind, 1))
        total = tp[kind, me[kind]].astype(F32)
        for i in range(4):
            total = total + tr[kind, i].astype(F32)
        tp[kind, me[kind]] = total.astype(BF16)

    stats_third()
    for dx, flip in GROUP:
        j = member(dx, flip)
        arrived(st_c.at[j], sc_rs.at[j], sibling)

    owners = [4 * (me[kind] % 2) + 2 * h + kind for kind in (0, 1) for h in (0, 1)]
    d_col[...] = jnp.concatenate([st_c[j] for j in owners] + [jnp.zeros((64, 128), F32)], axis=0).T
    for kind in (0, 1):
        for d in range(1, 8):
            src = (me[kind] + d) % 8
            arrived(r1.at[kind, src], d1_rs.at[kind, src], along(1 - kind, 1))
        info = d_col[pl.ds(pl.multiple_of(me[kind] // 2 * 16, 16), 16), :]
        for b in range(2):
            first = 32 * kind + 16 * b
            rows = info[:, first + 1 : first + 2] * tp[kind, me[kind], 16 * b : 16 * b + 16, :].astype(F32)
            for d in range(8):
                part = r1[kind, (me[kind] + 8 - d) % 8, 16 * b : 16 * b + 16, :].astype(F32)
                rows = rows + info[:, first + 8 + d : first + 9 + d] * part
            for q in range(2):
                low, high = pack(rows[8 * q : 8 * q + 8])
                s2[kind, 4 * b + 2 * q] = low.astype(BF16)
                s2[kind, 4 * b + 2 * q + 1] = high.astype(BF16)
        for d in FAR_FIRST:
            to = (me[1 - kind] + d) % 8
            c = remote(s2.at[kind, to], r2.at[kind, d], d2_ss.at[kind, d], d2_rs.at[kind, d], along(kind, d))
            c.start()
            sends.append(c)

    t_col[...] = st_c[...].reshape(128, 128).T

    def logit_grads(pair, _):
        column = (lax.broadcasted_iota(I32, (16, vocab), 1) + first_column).astype(F32)
        info = t_col[pl.ds(pl.multiple_of(pair * 16, 16), 16), :]
        for j in range(8):
            kind, x = j % 2, j // 2
            value = info[:, 16 * j : 16 * j + 1] * e_all[j, pair].astype(F32)
            value = jnp.where(column == info[:, 16 * j + 2 : 16 * j + 3], info[:, 16 * j + 1 : 16 * j + 2], value)
            g[kind, 2 * pair + x // 2, 16 * (x % 2) : 16 * (x % 2) + 16, :] = value.astype(BF16)
        return 0

    lax.fori_loop(0, 4, logit_grads, 0)

    def weight_tile(n, _):
        lanes = pl.ds(pl.multiple_of(n * 256, 256), 256)
        part = lax.dot_general(
            hid[:, :, :, lanes].reshape(512, 256), g[...].reshape(512, vocab), (((0,), (0,)), ((), ())),
            preferred_element_type=F32,
        )
        gw_ref[lanes, :] = part.astype(BF16)
        return 0

    lax.fori_loop(0, 4, weight_tile, 0)

    halves = []
    for kind in (0, 1):
        for d in FAR_FIRST:
            arrived(r2.at[kind, d], d2_rs.at[kind, d], along(kind, 1))
        halves.append(s2[kind, me[1 - kind]].astype(F32) + sum(r2[kind, d].astype(F32) for d in range(1, 8)))
    gh_ref[...] = unpack(*halves).astype(BF16)

    for c in sends:
        c.wait_send()


def body(hidden_states, weight, targets, upstream):
    vmem = pl.BlockSpec(memory_space=pltpu.VMEM)
    hbm = pl.BlockSpec(memory_space=pltpu.HBM)
    dma = pltpu.SemaphoreType.DMA
    scratch = [
        pltpu.VMEM((1024, 1024), BF16),
        pltpu.VMEM((1024, 1024), BF16),
        pltpu.VMEM((8, 1024), BF16),
        pltpu.VMEM((1, 512), I32),
        pltpu.VMEM((512,), BF16),
        pltpu.VMEM((2, 8, 32, 1024), BF16),
        pltpu.VMEM((2, 16, 256), BF16),
        pltpu.VMEM((2, 8, 16, 256), BF16),
        pltpu.VMEM((4, 64, 1024), F32),
        pltpu.VMEM((4, 64, 1024), F32),
        pltpu.VMEM((4, 64, 1024), F32),
        pltpu.VMEM((4, 64, 1024), F32),
        pltpu.VMEM((4, 3, 16, 1024), F32),
        pltpu.VMEM((8, 4, 16, 1024), BF16),
        pltpu.VMEM((2, 8, 32, 1024), BF16),
        pltpu.VMEM((2, 8, 32, 1024), BF16),
        pltpu.VMEM((2, 8, 32, 1024), BF16),
        pltpu.VMEM((2, 8, 16, 256), BF16),
        pltpu.VMEM((2, 8, 16, 256), BF16),
        pltpu.VMEM((2, 8, 32, 1024), BF16),
        pltpu.VMEM((2, 4, 32, 1024), BF16),
        pltpu.VMEM((2, 2, 32, 1024), BF16),
        pltpu.VMEM((2, 2, 16, 1024), BF16),
        pltpu.VMEM((128, 128), F32),
        pltpu.VMEM((512, 128), F32),
        pltpu.VMEM((128, 128), F32),
        pltpu.VMEM((8, 8, 128), F32),
        pltpu.VMEM((8, 8, 128), F32),
        pltpu.VMEM((8, 16, 128), F32),
        pltpu.VMEM((128, 128), F32),
        pltpu.VMEM((128, 128), F32),
        dma, dma((3,)),
        dma((2, 8)), dma((2, 8)), dma((2, 8)), dma((2, 8)), dma((2, 2)),
        dma((4,)), dma((4,)), dma((4, 3)), dma((4, 3)),
        dma((7, 4)), dma((8, 4)),
        dma((8,)), dma((8,)), dma((8,)), dma((8,)), dma((7,)), dma((8,)),
        dma((2, 8)), dma((2, 8)), dma((2, 8)), dma((2, 8)), dma((2, 8)), dma((2, 8)),
    ]
    operands = [
        pltpu.with_memory_space_constraint(a, pltpu.HBM)
        for a in (hidden_states, weight, targets.reshape(1, 512), upstream)
    ]
    return pl.pallas_call(
        kernel,
        out_shape=(
            jax.ShapeDtypeStruct(hidden_states.shape, BF16),
            jax.ShapeDtypeStruct(weight.shape, BF16),
        ),
        in_specs=[hbm, hbm, hbm, hbm],
        out_specs=(vmem, vmem),
        scratch_shapes=scratch,
        name="projection_backward",
        cost_estimate=pl.CostEstimate(flops=3 * 2 * 512 * 1024 * 1024, bytes_accessed=5 << 20, transcendentals=1 << 16),
        compiler_params=pltpu.CompilerParams(collective_id=0, has_side_effects=True, vmem_limit_bytes=48 << 20),
    )(*operands)


def solution(mesh):
    return jax.shard_map(
        body,
        mesh=mesh,
        in_specs=(P(("gx", "gy"), "gz"), P("gz", ("gx", "gy")), P(), P()),
        out_specs=(P(("gx", "gy"), "gz"), P("gz", ("gx", "gy"))),
        check_vma=False,
    )
```

```python
import functools

import jax
import jax.numpy as jnp
from jax import lax
from jax.experimental import pallas as pl
from jax.experimental.pallas import tpu as pltpu
from jax.sharding import PartitionSpec as P

MESH = pl.DeviceIdType.MESH
F32, BF16, I32 = jnp.float32, jnp.bfloat16, jnp.int32
FAR_FIRST = (4, 3, 5, 2, 6, 1, 7)
GROUP = ((2, 0), (2, 1), (1, 0), (3, 0), (1, 1), (3, 1), (0, 1))


def remote(src, dst, send_sem, recv_sem, device):
    return pltpu.make_async_remote_copy(
        src_ref=src, dst_ref=dst, send_sem=send_sem, recv_sem=recv_sem, device_id=device, device_id_type=MESH
    )


def upper_rows(shape):
    return lax.broadcasted_iota(I32, shape, 0) < 4


def pack(a):
    q = [a[:, 256 * k : 256 * (k + 1)] for k in range(4)]
    t = [pltpu.roll(x, 4, 0) for x in q]
    first = upper_rows((8, 256))
    low = jnp.concatenate([jnp.where(first, q[0], t[1]), jnp.where(first, q[2], t[3])], axis=0)
    high = jnp.concatenate([jnp.where(first, t[0], q[1]), jnp.where(first, t[2], q[3])], axis=0)
    return low, high


def unpack(low, high):
    first = upper_rows((8, 256))
    parts = []
    for k in range(2):
        a, c = low[8 * k : 8 * k + 8], high[8 * k : 8 * k + 8]
        parts.append(jnp.where(first, a, pltpu.roll(c, 4, 0)))
        parts.append(jnp.where(first, pltpu.roll(a, 4, 0), c))
    return jnp.concatenate(parts, axis=1)


def rows_of(*rows):
    sub = lax.broadcasted_iota(I32, (8, 128), 0)
    out = jnp.zeros((8, 128), F32)
    for k, row in enumerate(rows):
        out = jnp.where(sub == k, jnp.broadcast_to(row, (8, 128)), out)
    return out


def combine(stats):
    peaks = [stats[k, 0:1, :] for k in range(stats.shape[0])]
    peak = functools.reduce(jnp.maximum, peaks)
    scale = [jnp.exp(p - peak) for p in peaks]
    total = sum(stats[k, 1:2, :] * scale[k] for k in range(stats.shape[0]))
    chosen = sum(stats[k, 2:3, :] * scale[k] for k in range(stats.shape[0]))
    return peak, total, chosen


def kernel(
    h_hbm, w_hbm, tgt_hbm, up_hbm, gh_ref, gw_ref,
    w, wt, h_ref, tgt_ref, up_ref, hid, a1s, a1r, keep, cs, cr, xs, xr, e_all, g, p, r1, s2, r2,
    tp, tr, tg, th, own_col, all_col, stat_col, st_a, st_b, st_c, t_col, d_col,
    w_sem, in_sem, a1_ss, a1_rs, a2_ss, a2_rs, a2_hs, c_ss, c_rs, x_ss, x_rs,
    e_ss, e_rs, sa_ss, sa_rs, sb_ss, sb_rs, sc_ss, sc_rs, t_ss, t_rs, d1_ss, d1_rs, d2_ss, d2_rs,
):
    z, y, gz = lax.axis_index("gx"), lax.axis_index("gy"), lax.axis_index("gz")
    xx, core = gz // 2, gz % 2
    vocab = w.shape[1]
    zp, yp = z // 2, y // 2
    first_column = (z * 8 + y) * vocab
    contract = (((1,), (1,)), ((), ()))
    me = (z, y)

    def along(kind, d):
        return (z, (y + d) % 8, gz) if kind == 0 else ((z + d) % 8, y, gz)

    def member(dx, flip):
        c = 1 - core if flip else core
        return ((xx + dx) % 4) * 2 + c

    load_w = pltpu.make_async_copy(w_hbm, w, w_sem)
    load_w.start()
    loads = [
        pltpu.make_async_copy(src, dst, in_sem.at[i])
        for i, (src, dst) in enumerate(((h_hbm, h_ref), (tgt_hbm, tgt_ref), (up_hbm, up_ref)))
    ]
    for c in loads:
        c.start()

    barrier = pltpu.get_barrier_semaphore()
    for d in FAR_FIRST:
        for kind in (0, 1):
            pl.semaphore_signal(barrier, inc=1, device_id=along(kind, d), device_id_type=MESH)
    for dx, flip in GROUP:
        pl.semaphore_signal(barrier, inc=1, device_id=(z, y, member(dx, flip)), device_id_type=MESH)

    for c in loads:
        c.wait()
    low, high = pack(h_ref[...].astype(F32))
    a1s[0] = low.astype(BF16)
    a1s[1] = high.astype(BF16)
    a1r[0, y] = low.astype(BF16)
    a1r[1, z] = high.astype(BF16)

    pl.semaphore_wait(barrier, 21)

    sends = []
    for d in FAR_FIRST:
        for kind in (0, 1):
            c = remote(a1s.at[kind], a1r.at[kind, me[1 - kind]], a1_ss.at[kind, d], a1_rs.at[kind, me[1 - kind]], along(kind, d))
            c.start()
            sends.append(c)

    def arrived(dst, sem, peer):
        remote(dst, dst, sem, sem, peer).wait_recv()

    k = lax.broadcasted_iota(I32, (128, 512), 0)
    t = lax.broadcasted_iota(I32, (128, 512), 1)
    block = 2 * (k >> 4) + xx // 2
    other = (xx % 2) * 4 + ((k >> 2) & 3)
    zt = jnp.where(core == 0, block, other)
    yt = jnp.where(core == 0, other, block)
    token = zt * 64 + yt * 8 + core * 4 + (k & 3)
    select = jnp.where((token == t) & (k < 64), 1.0, 0.0).astype(BF16)
    tgt = tgt_ref[...]
    sub = lax.broadcasted_iota(I32, (128, 512), 0)
    values = jnp.where(sub == 0, jnp.broadcast_to((tgt >> 8).astype(F32), (128, 512)), 0.0)
    values = jnp.where(sub == 1, jnp.broadcast_to((tgt & 255).astype(F32), (128, 512)), values)
    values = jnp.where(sub == 2, jnp.broadcast_to(up_ref[...].reshape(1, 512).astype(F32), (128, 512)), values).astype(BF16)
    own_col[...] = lax.dot_general(select, values, contract, preferred_element_type=F32)
    own_row = lax.dot_general(values, select, contract, preferred_element_type=F32)
    tgt_row = own_row[0:1, :] * 256.0 + own_row[1:2, :]
    up_row = own_row[2:3, :]
    stat_col[...] = jnp.zeros((128, 128), F32)
    row = lax.broadcasted_iota(I32, (512, 128), 0)
    first, second = (row >> 5) & 7, (row & 31) >> 2
    token = jnp.where(row < 256, first * 64 + second * 8, second * 64 + first * 8 + 4) + (row & 3)
    order = (token[:, 0:1] == lax.broadcasted_iota(I32, (512, 512), 1)).astype(F32).astype(BF16)
    all_col[...] = lax.dot_general(order, values, contract, preferred_element_type=F32)
    load_w.wait()

    def turn(n, _):
        lanes = pl.ds(pl.multiple_of(n * 256, 256), 256)
        wt[:, lanes] = w[lanes, :].T
        return 0

    lax.fori_loop(0, 4, turn, 0)

    def chosen_rows(b, _):
        info = all_col[pl.ds(pl.multiple_of(b * 128, 128), 128), :]
        target = info[:, 0:1] * 256.0 + info[:, 1:2]
        hit = ((lax.broadcasted_iota(I32, (128, vocab), 1) + first_column).astype(F32) == target).astype(F32)
        part = jnp.dot(hit.astype(BF16), wt[...], preferred_element_type=F32).astype(BF16)
        tp[b // 2, pl.ds((b % 2) * 4, 4)] = part.reshape(4, 32, 1024)
        return 0

    lax.fori_loop(0, 4, chosen_rows, 0)

    def send_chosen(kind, src, dst, i, d):
        c = remote(src, dst, t_ss.at[kind, i], t_rs.at[kind, i], along(1 - kind, d))
        c.start()
        sends.append(c)

    def spread_chosen():
        for kind in (0, 1):
            for h, d in enumerate((1, 7)):
                half = pl.ds(16 * h, 16)
                send_chosen(kind, tp.at[kind, (me[kind] + 4) % 8, half], th.at[kind, h], 4 + h, 2 * d)
                send_chosen(kind, tp.at[kind, (me[kind] + 3 * d) % 8], tg.at[kind, h], 2 + h, d)
                send_chosen(kind, tp.at[kind, (me[kind] + d) % 8], tr.at[kind, h], h, d)

    def join_chosen():
        for kind in (0, 1):
            for h, d in enumerate((1, 7)):
                arrived(tg.at[kind, h], t_rs.at[kind, 2 + h], along(1 - kind, 1))
                arrived(th.at[kind, h], t_rs.at[kind, 4 + h], along(1 - kind, 1))
                q = (me[kind] + 2 * d) % 8
                for b in (0, 1):
                    rows = pl.ds(16 * b, 16)
                    total = tp[kind, q, rows, :].astype(F32) + tg[kind, h, rows, :].astype(F32)
                    if b == h:
                        total = total + th[kind, h].astype(F32)
                    tp[kind, q, rows, :] = total.astype(BF16)
                send_chosen(kind, tp.at[kind, q], tr.at[kind, 2 + h], 6 + h, 2 * d)

    for kind in (0, 1):
        mine = me[1 - kind]
        for d in range(1, 8):
            src = (mine + d) % 8
            arrived(a1r.at[kind, src], a1_rs.at[kind, src], along(kind, 1))
        for b in range(2):
            rows = [
                unpack(a1r[kind, 4 * b + 2 * q].astype(F32), a1r[kind, 4 * b + 2 * q + 1].astype(F32)) for q in range(2)
            ]
            hid[kind, me[kind], 16 * b : 16 * b + 16, :] = jnp.concatenate(rows, axis=0).astype(BF16)
        for d in (2, 6, 1, 7):
            slot = hid.at[kind, me[kind]]
            c = remote(slot, slot, a2_ss.at[kind, d], a2_rs.at[kind, me[kind]], along(1 - kind, d))
            c.start()
            sends.append(c)

    def shift(s, parity):
        return (0, 2 * parity + 3, 5 - 2 * parity, 2)[s]

    def pair_of(kind, s):
        return (zp + shift(s, z % 2)) % 4 if kind == 0 else (yp + shift(s, y % 2)) % 4

    def own_pair(s):
        return jnp.where(core == 0, pair_of(0, s), pair_of(1, s))

    def other_pair(s):
        return jnp.where(core == 0, pair_of(1, s), pair_of(0, s))

    sibling = (z, y, member(0, 1))

    def relay():
        for kind in (0, 1):
            for h, d in enumerate((1, 7)):
                q = (me[kind] - 2 * d) % 8
                slot = hid.at[kind, q]
                arrived(slot, a2_rs.at[kind, q], along(1 - kind, 1))
                c = remote(slot, slot, a2_ss.at[kind, 3 + 2 * h], a2_rs.at[kind, q], along(1 - kind, d))
                c.start()
                sends.append(c)
                half = hid.at[kind, q, 16 * h : 16 * h + 16]
                c = remote(half, half, a2_ss.at[kind, 4 * h], a2_hs.at[kind, h], along(1 - kind, 2 * d))
                c.start()
                sends.append(c)

    def multiply(s):
        for kind in (0, 1):
            q = 2 * pair_of(kind, s) + 1 - me[kind] % 2
            arrived(hid.at[kind, q], a2_rs.at[kind, q], along(1 - kind, 1))
            if s == 3:
                q = (me[kind] + 4) % 8
                for h in (0, 1):
                    arrived(hid.at[kind, q, 16 * h : 16 * h + 16], a2_hs.at[kind, h], along(1 - kind, 1))
        mine, others = own_pair(s), other_pair(s)

        lhs = jnp.concatenate(
            [hid[core, pl.ds(2 * mine, 2)].reshape(64, 1024), hid[1 - core, pl.ds(2 * others, 2)].reshape(64, 1024)], axis=0
        )
        part = jnp.dot(lhs, w[...], preferred_element_type=F32)
        cs[s] = part[64:]
        keep[s] = part[:64]
        c = remote(cs.at[s], cr.at[s], c_ss.at[s], c_rs.at[s], sibling)
        c.start()
        sends.append(c)

    def pass_on(s):
        arrived(cr.at[s], c_rs.at[s], sibling)
        xs[s] = keep[s] + cr[s]
        for dx in (2, 1, 3):
            to = (xx + dx) % 4
            c = remote(
                xs.at[s, pl.ds(pl.multiple_of(to * 16, 16), 16)], xr.at[s, dx - 1], x_ss.at[s, dx - 1], x_rs.at[s, dx - 1],
                (z, y, member(dx, 0)),
            )
            c.start()
            sends.append(c)

    def finish(s):
        for dx in (2, 1, 3):
            arrived(xr.at[s, dx - 1], x_rs.at[s, dx - 1], sibling)
        pair = own_pair(s)
        logits = xs[s, pl.ds(pl.multiple_of(xx * 16, 16), 16), :] + xr[s, 0] + xr[s, 1] + xr[s, 2]
        rows = pl.ds(pl.multiple_of(pair * 16, 16), 16)
        info = own_col[rows, :]
        target = info[:, 0:1] * 256.0 + info[:, 1:2]
        column = lax.broadcasted_iota(I32, (16, vocab), 1) + first_column
        hit = column.astype(F32) == target
        peak = jnp.max(logits, axis=1, keepdims=True)
        value = jnp.exp(logits - peak)
        rest = jnp.where(hit, 0.0, value)
        e_all[gz, pair] = rest.astype(BF16)
        for dx in (2, 1, 3):
            share(gz, pair, s, dx, member(dx, 0))
        share(gz, pair, s, 0, member(0, 1))
        total = jnp.sum(rest, axis=1, keepdims=True)
        chosen = jnp.sum(jnp.where(hit, value, 0.0), axis=1, keepdims=True)
        lane = lax.broadcasted_iota(I32, (16, 128), 1)
        stat_col[rows, :] = jnp.where(lane == 0, peak, jnp.where(lane == 1, total, jnp.where(lane == 2, chosen, 0.0)))

    def share(j, pair, s, i, to):
        slot = e_all.at[j, pair]
        c = remote(slot, slot, e_ss.at[i, s], e_rs.at[j, pair], (z, y, to))
        c.start()
        sends.append(c)

    def forward(s):
        for dx in (1, 3, 2):
            j, pair = member(dx, 0), own_pair(s)
            arrived(e_all.at[j, pair], e_rs.at[j, pair], sibling)
            share(j, pair, s, 3 + dx, member(0, 1))

    def scatter(kind, s):
        pair = pair_of(kind, s)
        if s == 0:
            chunks = [4 * pair + 1 - me[kind]]
            r1[kind, me[kind]] = p[kind, me[kind]]
        else:
            chunks = [2 * pair, 2 * pair + 1]
        for i, q in enumerate(chunks):
            to = (q, y, gz) if kind == 0 else (z, q, gz)
            c = remote(
                p.at[kind, q], r1.at[kind, me[kind]], d1_ss.at[kind, 2 * s + i], d1_rs.at[kind, me[kind]], to
            )
            c.start()
            sends.append(c)

    def terms(s):
        pairs = (pair_of(0, s), pair_of(1, s))
        for dx in range(4):
            j, pair = member(dx, 1), other_pair(s)
            arrived(e_all.at[j, pair], e_rs.at[j, pair], sibling)
        lhs = jnp.concatenate([e_all[2 * x + kind, pairs[kind]] for kind in (0, 1) for x in range(4)], axis=0)
        part = jnp.dot(lhs, wt[...], preferred_element_type=F32).astype(BF16)
        for kind in (0, 1):
            p[kind, pl.ds(2 * pairs[kind], 2)] = part[64 * kind : 64 * kind + 64].reshape(2, 32, 1024)
            scatter(kind, s)

    def stat_peer(phase, d):
        over_z = core == phase
        return (jnp.where(over_z, (z + d) % 8, z), jnp.where(over_z, y, (y + d) % 8), gz)

    def give(buf, ss, rs, phase):
        for d in FAR_FIRST:
            c = remote(buf.at[0], buf.at[d], ss.at[d], rs.at[d], stat_peer(phase, d))
            c.start()
            sends.append(c)

    def take(buf, rs, phase):
        for d in FAR_FIRST:
            arrived(buf.at[d], rs.at[d], stat_peer(phase, d))
        return combine(buf[...])

    def stats_first():
        st_a[0] = stat_col[...].T[0:8, :]
        give(st_a, sa_ss, sa_rs, 0)

    def stats_second():
        st_b[0] = rows_of(*take(st_a, sa_rs, 0))
        give(st_b, sb_ss, sb_rs, 1)

    def stats_third():
        peak, total, chosen = take(st_b, sb_rs, 1)
        used = lax.broadcasted_iota(I32, (1, 128), 1) < 64
        scale = up_row / jnp.where(used, total + chosen, 1.0)
        factors = [scale * jnp.exp(st_a[d, 0:1, :] - peak) for d in range(8)]
        st_c[gz, 0:8] = rows_of(factors[0], -scale * total, tgt_row)
        st_c[gz, 8:16] = rows_of(*factors)
        for i, (dx, flip) in enumerate(GROUP):
            c = remote(st_c.at[gz], st_c.at[gz], sc_ss.at[i], sc_rs.at[gz], (z, y, member(dx, flip)))
            c.start()
            sends.append(c)

    multiply(0)
    relay()
    pass_on(0)
    multiply(1)
    pass_on(1)
    finish(0)
    multiply(2)
    pass_on(2)
    finish(1)
    forward(0)
    multiply(3)
    spread_chosen()
    pass_on(3)
    finish(2)
    terms(0)
    forward(1)
    terms(1)
    finish(3)
    stats_first()
    join_chosen()
    forward(2)
    terms(2)
    stats_second()
    forward(3)
    terms(3)

    for kind in (0, 1):
        for i in (0, 1, 2, 3):
            arrived(tr.at[kind, i], t_rs.at[kind, (0, 1, 6, 7)[i]], along(1 - kind, 1))
        total = tp[kind, me[kind]].astype(F32)
        for i in range(4):
            total = total + tr[kind, i].astype(F32)
        tp[kind, me[kind]] = total.astype(BF16)

    stats_third()
    for dx, flip in GROUP:
        j = member(dx, flip)
        arrived(st_c.at[j], sc_rs.at[j], sibling)

    owners = [4 * (me[kind] % 2) + 2 * h + kind for kind in (0, 1) for h in (0, 1)]
    d_col[...] = jnp.concatenate([st_c[j] for j in owners] + [jnp.zeros((64, 128), F32)], axis=0).T
    for kind in (0, 1):
        for d in range(1, 8):
            src = (me[kind] + d) % 8
            arrived(r1.at[kind, src], d1_rs.at[kind, src], along(1 - kind, 1))
        info = d_col[pl.ds(pl.multiple_of(me[kind] // 2 * 16, 16), 16), :]
        for b in range(2):
            first = 32 * kind + 16 * b
            rows = info[:, first + 1 : first + 2] * tp[kind, me[kind], 16 * b : 16 * b + 16, :].astype(F32)
            for d in range(8):
                part = r1[kind, (me[kind] + 8 - d) % 8, 16 * b : 16 * b + 16, :].astype(F32)
                rows = rows + info[:, first + 8 + d : first + 9 + d] * part
            for q in range(2):
                low, high = pack(rows[8 * q : 8 * q + 8])
                s2[kind, 4 * b + 2 * q] = low.astype(BF16)
                s2[kind, 4 * b + 2 * q + 1] = high.astype(BF16)
        for d in FAR_FIRST:
            to = (me[1 - kind] + d) % 8
            c = remote(s2.at[kind, to], r2.at[kind, d], d2_ss.at[kind, d], d2_rs.at[kind, d], along(kind, d))
            c.start()
            sends.append(c)

    t_col[...] = st_c[...].reshape(128, 128).T

    def logit_grads(pair, _):
        column = (lax.broadcasted_iota(I32, (16, vocab), 1) + first_column).astype(F32)
        info = t_col[pl.ds(pl.multiple_of(pair * 16, 16), 16), :]
        for j in range(8):
            kind, x = j % 2, j // 2
            value = info[:, 16 * j : 16 * j + 1] * e_all[j, pair].astype(F32)
            value = jnp.where(column == info[:, 16 * j + 2 : 16 * j + 3], info[:, 16 * j + 1 : 16 * j + 2], value)
            g[kind, 2 * pair + x // 2, 16 * (x % 2) : 16 * (x % 2) + 16, :] = value.astype(BF16)
        return 0

    lax.fori_loop(0, 4, logit_grads, 0)

    def weight_tile(n, _):
        lanes = pl.ds(pl.multiple_of(n * 256, 256), 256)
        part = lax.dot_general(
            hid[:, :, :, lanes].reshape(512, 256), g[...].reshape(512, vocab), (((0,), (0,)), ((), ())),
            preferred_element_type=F32,
        )
        gw_ref[lanes, :] = part.astype(BF16)
        return 0

    lax.fori_loop(0, 4, weight_tile, 0)

    halves = []
    for kind in (0, 1):
        for d in FAR_FIRST:
            arrived(r2.at[kind, d], d2_rs.at[kind, d], along(kind, 1))
        halves.append(s2[kind, me[1 - kind]].astype(F32) + sum(r2[kind, d].astype(F32) for d in range(1, 8)))
    gh_ref[...] = unpack(*halves).astype(BF16)

    for c in sends:
        c.wait_send()


def body(hidden_states, weight, targets, upstream):
    vmem = pl.BlockSpec(memory_space=pltpu.VMEM)
    hbm = pl.BlockSpec(memory_space=pltpu.HBM)
    dma = pltpu.SemaphoreType.DMA
    scratch = [
        pltpu.VMEM((1024, 1024), BF16),
        pltpu.VMEM((1024, 1024), BF16),
        pltpu.VMEM((8, 1024), BF16),
        pltpu.VMEM((1, 512), I32),
        pltpu.VMEM((512,), BF16),
        pltpu.VMEM((2, 8, 32, 1024), BF16),
        pltpu.VMEM((2, 16, 256), BF16),
        pltpu.VMEM((2, 8, 16, 256), BF16),
        pltpu.VMEM((4, 64, 1024), F32),
        pltpu.VMEM((4, 64, 1024), F32),
        pltpu.VMEM((4, 64, 1024), F32),
        pltpu.VMEM((4, 64, 1024), F32),
        pltpu.VMEM((4, 3, 16, 1024), F32),
        pltpu.VMEM((8, 4, 16, 1024), BF16),
        pltpu.VMEM((2, 8, 32, 1024), BF16),
        pltpu.VMEM((2, 8, 32, 1024), BF16),
        pltpu.VMEM((2, 8, 32, 1024), BF16),
        pltpu.VMEM((2, 8, 16, 256), BF16),
        pltpu.VMEM((2, 8, 16, 256), BF16),
        pltpu.VMEM((2, 8, 32, 1024), BF16),
        pltpu.VMEM((2, 4, 32, 1024), BF16),
        pltpu.VMEM((2, 2, 32, 1024), BF16),
        pltpu.VMEM((2, 2, 16, 1024), BF16),
        pltpu.VMEM((128, 128), F32),
        pltpu.VMEM((512, 128), F32),
        pltpu.VMEM((128, 128), F32),
        pltpu.VMEM((8, 8, 128), F32),
        pltpu.VMEM((8, 8, 128), F32),
        pltpu.VMEM((8, 16, 128), F32),
        pltpu.VMEM((128, 128), F32),
        pltpu.VMEM((128, 128), F32),
        dma, dma((3,)),
        dma((2, 8)), dma((2, 8)), dma((2, 8)), dma((2, 8)), dma((2, 2)),
        dma((4,)), dma((4,)), dma((4, 3)), dma((4, 3)),
        dma((7, 4)), dma((8, 4)),
        dma((8,)), dma((8,)), dma((8,)), dma((8,)), dma((7,)), dma((8,)),
        dma((2, 8)), dma((2, 8)), dma((2, 8)), dma((2, 8)), dma((2, 8)), dma((2, 8)),
    ]
    operands = [
        pltpu.with_memory_space_constraint(a, pltpu.HBM)
        for a in (hidden_states, weight, targets.reshape(1, 512), upstream)
    ]
    return pl.pallas_call(
        kernel,
        out_shape=(
            jax.ShapeDtypeStruct(hidden_states.shape, BF16),
            jax.ShapeDtypeStruct(weight.shape, BF16),
        ),
        in_specs=[hbm, hbm, hbm, hbm],
        out_specs=(vmem, vmem),
        scratch_shapes=scratch,
        name="projection_backward",
        cost_estimate=pl.CostEstimate(flops=3 * 2 * 512 * 1024 * 1024, bytes_accessed=5 << 20, transcendentals=1 << 16),
        compiler_params=pltpu.CompilerParams(collective_id=0, has_side_effects=True, vmem_limit_bytes=48 << 20),
    )(*operands)


def solution(mesh):
    return jax.shard_map(
        body,
        mesh=mesh,
        in_specs=(P(("gx", "gy"), "gz"), P("gz", ("gx", "gy")), P(), P()),
        out_specs=(P(("gx", "gy"), "gz"), P("gz", ("gx", "gy"))),
        check_vma=False,
    )
```

```python
import functools

import jax
import jax.numpy as jnp
from jax import lax
from jax.experimental import pallas as pl
from jax.experimental.pallas import tpu as pltpu
from jax.sharding import PartitionSpec as P

MESH = pl.DeviceIdType.MESH
F32, BF16, I32 = jnp.float32, jnp.bfloat16, jnp.int32
FAR_FIRST = (4, 3, 5, 2, 6, 1, 7)
GROUP = ((2, 0), (2, 1), (1, 0), (3, 0), (1, 1), (3, 1), (0, 1))


def remote(src, dst, send_sem, recv_sem, device):
    return pltpu.make_async_remote_copy(
        src_ref=src, dst_ref=dst, send_sem=send_sem, recv_sem=recv_sem, device_id=device, device_id_type=MESH
    )


def upper_rows(shape):
    return lax.broadcasted_iota(I32, shape, 0) < 4


def pack(a):
    q = [a[:, 256 * k : 256 * (k + 1)] for k in range(4)]
    t = [pltpu.roll(x, 4, 0) for x in q]
    first = upper_rows((8, 256))
    low = jnp.concatenate([jnp.where(first, q[0], t[1]), jnp.where(first, q[2], t[3])], axis=0)
    high = jnp.concatenate([jnp.where(first, t[0], q[1]), jnp.where(first, t[2], q[3])], axis=0)
    return low, high


def unpack(low, high):
    first = upper_rows((8, 256))
    parts = []
    for k in range(2):
        a, c = low[8 * k : 8 * k + 8], high[8 * k : 8 * k + 8]
        parts.append(jnp.where(first, a, pltpu.roll(c, 4, 0)))
        parts.append(jnp.where(first, pltpu.roll(a, 4, 0), c))
    return jnp.concatenate(parts, axis=1)


def rows_of(*rows):
    sub = lax.broadcasted_iota(I32, (8, 128), 0)
    out = jnp.zeros((8, 128), F32)
    for k, row in enumerate(rows):
        out = jnp.where(sub == k, jnp.broadcast_to(row, (8, 128)), out)
    return out


def combine(stats):
    peaks = [stats[k, 0:1, :] for k in range(stats.shape[0])]
    peak = functools.reduce(jnp.maximum, peaks)
    scale = [jnp.exp(p - peak) for p in peaks]
    total = sum(stats[k, 1:2, :] * scale[k] for k in range(stats.shape[0]))
    chosen = sum(stats[k, 2:3, :] * scale[k] for k in range(stats.shape[0]))
    return peak, total, chosen


def kernel(
    h_hbm, w_hbm, tgt_hbm, up_hbm, gh_ref, gw_ref,
    w, wt, h_ref, tgt_ref, up_ref, hid, a1s, a1r, keep, cs, cr, xs, xr, e_all, g, p, r1, s2, r2,
    tp, tr, tg, th, own_col, all_col, stat_col, st_a, st_b, st_c, t_col, d_col,
    w_sem, in_sem, a1_ss, a1_rs, a2_ss, a2_rs, a2_hs, c_ss, c_rs, x_ss, x_rs,
    e_ss, e_rs, sa_ss, sa_rs, sb_ss, sb_rs, sc_ss, sc_rs, t_ss, t_rs, d1_ss, d1_rs, d2_ss, d2_rs,
):
    z, y, gz = lax.axis_index("gx"), lax.axis_index("gy"), lax.axis_index("gz")
    xx, core = gz // 2, gz % 2
    vocab = w.shape[1]
    zp, yp = z // 2, y // 2
    first_column = (z * 8 + y) * vocab
    contract = (((1,), (1,)), ((), ()))
    me = (z, y)

    def along(kind, d):
        return (z, (y + d) % 8, gz) if kind == 0 else ((z + d) % 8, y, gz)

    def member(dx, flip):
        c = 1 - core if flip else core
        return ((xx + dx) % 4) * 2 + c

    load_w = pltpu.make_async_copy(w_hbm, w, w_sem)
    load_w.start()
    loads = [
        pltpu.make_async_copy(src, dst, in_sem.at[i])
        for i, (src, dst) in enumerate(((h_hbm, h_ref), (tgt_hbm, tgt_ref), (up_hbm, up_ref)))
    ]
    for c in loads:
        c.start()

    barrier = pltpu.get_barrier_semaphore()
    for d in FAR_FIRST:
        for kind in (0, 1):
            pl.semaphore_signal(barrier, inc=1, device_id=along(kind, d), device_id_type=MESH)
    for dx, flip in GROUP:
        pl.semaphore_signal(barrier, inc=1, device_id=(z, y, member(dx, flip)), device_id_type=MESH)

    for c in loads:
        c.wait()
    low, high = pack(h_ref[...].astype(F32))
    a1s[0] = low.astype(BF16)
    a1s[1] = high.astype(BF16)
    a1r[0, y] = low.astype(BF16)
    a1r[1, z] = high.astype(BF16)

    pl.semaphore_wait(barrier, 21)

    sends = []
    for d in FAR_FIRST:
        for kind in (0, 1):
            c = remote(a1s.at[kind], a1r.at[kind, me[1 - kind]], a1_ss.at[kind, d], a1_rs.at[kind, me[1 - kind]], along(kind, d))
            c.start()
            sends.append(c)

    def arrived(dst, sem, peer):
        remote(dst, dst, sem, sem, peer).wait_recv()

    k = lax.broadcasted_iota(I32, (128, 512), 0)
    t = lax.broadcasted_iota(I32, (128, 512), 1)
    block = 2 * (k >> 4) + xx // 2
    other = (xx % 2) * 4 + ((k >> 2) & 3)
    zt = jnp.where(core == 0, block, other)
    yt = jnp.where(core == 0, other, block)
    token = zt * 64 + yt * 8 + core * 4 + (k & 3)
    select = jnp.where((token == t) & (k < 64), 1.0, 0.0).astype(BF16)
    tgt = tgt_ref[...]
    sub = lax.broadcasted_iota(I32, (128, 512), 0)
    values = jnp.where(sub == 0, jnp.broadcast_to((tgt >> 8).astype(F32), (128, 512)), 0.0)
    values = jnp.where(sub == 1, jnp.broadcast_to((tgt & 255).astype(F32), (128, 512)), values)
    values = jnp.where(sub == 2, jnp.broadcast_to(up_ref[...].reshape(1, 512).astype(F32), (128, 512)), values).astype(BF16)
    own_col[...] = lax.dot_general(select, values, contract, preferred_element_type=F32)
    own_row = lax.dot_general(values, select, contract, preferred_element_type=F32)
    tgt_row = own_row[0:1, :] * 256.0 + own_row[1:2, :]
    up_row = own_row[2:3, :]
    stat_col[...] = jnp.zeros((128, 128), F32)
    row = lax.broadcasted_iota(I32, (512, 128), 0)
    first, second = (row >> 5) & 7, (row & 31) >> 2
    token = jnp.where(row < 256, first * 64 + second * 8, second * 64 + first * 8 + 4) + (row & 3)
    order = (token[:, 0:1] == lax.broadcasted_iota(I32, (512, 512), 1)).astype(F32).astype(BF16)
    all_col[...] = lax.dot_general(order, values, contract, preferred_element_type=F32)
    load_w.wait()

    def turn(n, _):
        lanes = pl.ds(pl.multiple_of(n * 256, 256), 256)
        wt[:, lanes] = w[lanes, :].T
        return 0

    lax.fori_loop(0, 4, turn, 0)

    def chosen_rows(b, _):
        info = all_col[pl.ds(pl.multiple_of(b * 128, 128), 128), :]
        target = info[:, 0:1] * 256.0 + info[:, 1:2]
        hit = ((lax.broadcasted_iota(I32, (128, vocab), 1) + first_column).astype(F32) == target).astype(F32)
        part = jnp.dot(hit.astype(BF16), wt[...], preferred_element_type=F32).astype(BF16)
        tp[b // 2, pl.ds((b % 2) * 4, 4)] = part.reshape(4, 32, 1024)
        return 0

    lax.fori_loop(0, 4, chosen_rows, 0)

    def send_chosen(kind, src, dst, i, d):
        c = remote(src, dst, t_ss.at[kind, i], t_rs.at[kind, i], along(1 - kind, d))
        c.start()
        sends.append(c)

    def spread_chosen():
        for kind in (0, 1):
            for h, d in enumerate((1, 7)):
                half = pl.ds(16 * h, 16)
                send_chosen(kind, tp.at[kind, (me[kind] + 4) % 8, half], th.at[kind, h], 4 + h, 2 * d)
                send_chosen(kind, tp.at[kind, (me[kind] + 3 * d) % 8], tg.at[kind, h], 2 + h, d)
                send_chosen(kind, tp.at[kind, (me[kind] + d) % 8], tr.at[kind, h], h, d)

    def join_chosen():
        for kind in (0, 1):
            for h, d in enumerate((1, 7)):
                arrived(tg.at[kind, h], t_rs.at[kind, 2 + h], along(1 - kind, 1))
                arrived(th.at[kind, h], t_rs.at[kind, 4 + h], along(1 - kind, 1))
                q = (me[kind] + 2 * d) % 8
                for b in (0, 1):
                    rows = pl.ds(16 * b, 16)
                    total = tp[kind, q, rows, :].astype(F32) + tg[kind, h, rows, :].astype(F32)
                    if b == h:
                        total = total + th[kind, h].astype(F32)
                    tp[kind, q, rows, :] = total.astype(BF16)
                send_chosen(kind, tp.at[kind, q], tr.at[kind, 2 + h], 6 + h, 2 * d)

    for kind in (0, 1):
        mine = me[1 - kind]
        for d in range(1, 8):
            src = (mine + d) % 8
            arrived(a1r.at[kind, src], a1_rs.at[kind, src], along(kind, 1))
        for b in range(2):
            rows = [
                unpack(a1r[kind, 4 * b + 2 * q].astype(F32), a1r[kind, 4 * b + 2 * q + 1].astype(F32)) for q in range(2)
            ]
            hid[kind, me[kind], 16 * b : 16 * b + 16, :] = jnp.concatenate(rows, axis=0).astype(BF16)
        for d in (2, 6, 1, 7):
            slot = hid.at[kind, me[kind]]
            c = remote(slot, slot, a2_ss.at[kind, d], a2_rs.at[kind, me[kind]], along(1 - kind, d))
            c.start()
            sends.append(c)

    def shift(s, parity):
        return (0, 2 * parity + 3, 5 - 2 * parity, 2)[s]

    def pair_of(kind, s):
        return (zp + shift(s, z % 2)) % 4 if kind == 0 else (yp + shift(s, y % 2)) % 4

    def own_pair(s):
        return jnp.where(core == 0, pair_of(0, s), pair_of(1, s))

    def other_pair(s):
        return jnp.where(core == 0, pair_of(1, s), pair_of(0, s))

    sibling = (z, y, member(0, 1))

    def relay():
        for kind in (0, 1):
            for h, d in enumerate((1, 7)):
                q = (me[kind] - 2 * d) % 8
                slot = hid.at[kind, q]
                arrived(slot, a2_rs.at[kind, q], along(1 - kind, 1))
                c = remote(slot, slot, a2_ss.at[kind, 3 + 2 * h], a2_rs.at[kind, q], along(1 - kind, d))
                c.start()
                sends.append(c)
                half = hid.at[kind, q, 16 * h : 16 * h + 16]
                c = remote(half, half, a2_ss.at[kind, 4 * h], a2_hs.at[kind, h], along(1 - kind, 2 * d))
                c.start()
                sends.append(c)

    def multiply(s):
        for kind in (0, 1):
            q = 2 * pair_of(kind, s) + 1 - me[kind] % 2
            arrived(hid.at[kind, q], a2_rs.at[kind, q], along(1 - kind, 1))
            if s == 3:
                q = (me[kind] + 4) % 8
                for h in (0, 1):
                    arrived(hid.at[kind, q, 16 * h : 16 * h + 16], a2_hs.at[kind, h], along(1 - kind, 1))
        mine, others = own_pair(s), other_pair(s)

        lhs = jnp.concatenate(
            [hid[core, pl.ds(2 * mine, 2)].reshape(64, 1024), hid[1 - core, pl.ds(2 * others, 2)].reshape(64, 1024)], axis=0
        )
        part = jnp.dot(lhs, w[...], preferred_element_type=F32)
        cs[s] = part[64:]
        c = remote(cs.at[s], cr.at[s], c_ss.at[s], c_rs.at[s], sibling)
        c.start()
        sends.append(c)
        keep[s] = part[:64]

    def pass_on(s):
        arrived(cr.at[s], c_rs.at[s], sibling)
        for dx in (2, 1, 3, 0):
            rows = pl.ds(pl.multiple_of((xx + dx) % 4 * 16, 16), 16)
            xs[s, rows, :] = keep[s, rows, :] + cr[s, rows, :]
            if dx:
                c = remote(
                    xs.at[s, rows], xr.at[s, dx - 1], x_ss.at[s, dx - 1], x_rs.at[s, dx - 1], (z, y, member(dx, 0))
                )
                c.start()
                sends.append(c)

    def finish(s):
        for dx in (2, 1, 3):
            arrived(xr.at[s, dx - 1], x_rs.at[s, dx - 1], sibling)
        pair = own_pair(s)
        logits = xs[s, pl.ds(pl.multiple_of(xx * 16, 16), 16), :] + xr[s, 0] + xr[s, 1] + xr[s, 2]
        rows = pl.ds(pl.multiple_of(pair * 16, 16), 16)
        info = own_col[rows, :]
        target = info[:, 0:1] * 256.0 + info[:, 1:2]
        column = lax.broadcasted_iota(I32, (16, vocab), 1) + first_column
        hit = column.astype(F32) == target
        peak = jnp.max(logits, axis=1, keepdims=True)
        value = jnp.exp(logits - peak)
        rest = jnp.where(hit, 0.0, value)
        e_all[gz, pair] = rest.astype(BF16)
        for dx in (2, 1, 3):
            share(gz, pair, s, dx, member(dx, 0))
        share(gz, pair, s, 0, member(0, 1))
        total = jnp.sum(rest, axis=1, keepdims=True)
        chosen = jnp.sum(jnp.where(hit, value, 0.0), axis=1, keepdims=True)
        lane = lax.broadcasted_iota(I32, (16, 128), 1)
        stat_col[rows, :] = jnp.where(lane == 0, peak, jnp.where(lane == 1, total, jnp.where(lane == 2, chosen, 0.0)))

    def share(j, pair, s, i, to):
        slot = e_all.at[j, pair]
        c = remote(slot, slot, e_ss.at[i, s], e_rs.at[j, pair], (z, y, to))
        c.start()
        sends.append(c)

    def forward(s):
        for dx in (1, 3, 2):
            j, pair = member(dx, 0), own_pair(s)
            arrived(e_all.at[j, pair], e_rs.at[j, pair], sibling)
            share(j, pair, s, 3 + dx, member(0, 1))

    def scatter(kind, s):
        pair = pair_of(kind, s)
        if s == 0:
            chunks = [4 * pair + 1 - me[kind]]
            r1[kind, me[kind]] = p[kind, me[kind]]
        else:
            chunks = [2 * pair, 2 * pair + 1]
        for i, q in enumerate(chunks):
            to = (q, y, gz) if kind == 0 else (z, q, gz)
            c = remote(
                p.at[kind, q], r1.at[kind, me[kind]], d1_ss.at[kind, 2 * s + i], d1_rs.at[kind, me[kind]], to
            )
            c.start()
            sends.append(c)

    def terms(s):
        pairs = (pair_of(0, s), pair_of(1, s))
        for dx in range(4):
            j, pair = member(dx, 1), other_pair(s)
            arrived(e_all.at[j, pair], e_rs.at[j, pair], sibling)
        lhs = jnp.concatenate([e_all[2 * x + kind, pairs[kind]] for kind in (0, 1) for x in range(4)], axis=0)
        part = jnp.dot(lhs, wt[...], preferred_element_type=F32).astype(BF16)
        for kind in (0, 1):
            p[kind, pl.ds(2 * pairs[kind], 2)] = part[64 * kind : 64 * kind + 64].reshape(2, 32, 1024)
            scatter(kind, s)

    def stat_peer(phase, d):
        over_z = core == phase
        return (jnp.where(over_z, (z + d) % 8, z), jnp.where(over_z, y, (y + d) % 8), gz)

    def give(buf, ss, rs, phase):
        for d in FAR_FIRST:
            c = remote(buf.at[0], buf.at[d], ss.at[d], rs.at[d], stat_peer(phase, d))
            c.start()
            sends.append(c)

    def take(buf, rs, phase):
        for d in FAR_FIRST:
            arrived(buf.at[d], rs.at[d], stat_peer(phase, d))
        return combine(buf[...])

    def stats_first():
        st_a[0] = stat_col[...].T[0:8, :]
        give(st_a, sa_ss, sa_rs, 0)

    def stats_second():
        st_b[0] = rows_of(*take(st_a, sa_rs, 0))
        give(st_b, sb_ss, sb_rs, 1)

    def stats_third():
        peak, total, chosen = take(st_b, sb_rs, 1)
        used = lax.broadcasted_iota(I32, (1, 128), 1) < 64
        scale = up_row / jnp.where(used, total + chosen, 1.0)
        factors = [scale * jnp.exp(st_a[d, 0:1, :] - peak) for d in range(8)]
        st_c[gz, 0:8] = rows_of(factors[0], -scale * total, tgt_row)
        st_c[gz, 8:16] = rows_of(*factors)
        for i, (dx, flip) in enumerate(GROUP):
            c = remote(st_c.at[gz], st_c.at[gz], sc_ss.at[i], sc_rs.at[gz], (z, y, member(dx, flip)))
            c.start()
            sends.append(c)

    multiply(0)
    relay()
    pass_on(0)
    multiply(1)
    pass_on(1)
    finish(0)
    multiply(2)
    pass_on(2)
    finish(1)
    forward(0)
    multiply(3)
    spread_chosen()
    pass_on(3)
    finish(2)
    terms(0)
    forward(1)
    terms(1)
    finish(3)
    stats_first()
    forward(2)
    join_chosen()
    terms(2)
    stats_second()
    forward(3)
    terms(3)

    stats_third()

    for kind in (0, 1):
        for i in (0, 1, 2, 3):
            arrived(tr.at[kind, i], t_rs.at[kind, (0, 1, 6, 7)[i]], along(1 - kind, 1))
        total = tp[kind, me[kind]].astype(F32)
        for i in range(4):
            total = total + tr[kind, i].astype(F32)
        tp[kind, me[kind]] = total.astype(BF16)

    for dx, flip in GROUP:
        j = member(dx, flip)
        arrived(st_c.at[j], sc_rs.at[j], sibling)

    owners = [4 * (me[kind] % 2) + 2 * h + kind for kind in (0, 1) for h in (0, 1)]
    d_col[...] = jnp.concatenate([st_c[j] for j in owners] + [jnp.zeros((64, 128), F32)], axis=0).T
    for kind in (0, 1):
        for d in range(1, 8):
            src = (me[kind] + d) % 8
            arrived(r1.at[kind, src], d1_rs.at[kind, src], along(1 - kind, 1))
        info = d_col[pl.ds(pl.multiple_of(me[kind] // 2 * 16, 16), 16), :]
        for b in range(2):
            first = 32 * kind + 16 * b
            rows = info[:, first + 1 : first + 2] * tp[kind, me[kind], 16 * b : 16 * b + 16, :].astype(F32)
            for d in range(8):
                part = r1[kind, (me[kind] + 8 - d) % 8, 16 * b : 16 * b + 16, :].astype(F32)
                rows = rows + info[:, first + 8 + d : first + 9 + d] * part
            for q in range(2):
                low, high = pack(rows[8 * q : 8 * q + 8])
                s2[kind, 4 * b + 2 * q] = low.astype(BF16)
                s2[kind, 4 * b + 2 * q + 1] = high.astype(BF16)
        for d in FAR_FIRST:
            to = (me[1 - kind] + d) % 8
            c = remote(s2.at[kind, to], r2.at[kind, d], d2_ss.at[kind, d], d2_rs.at[kind, d], along(kind, d))
            c.start()
            sends.append(c)

    t_col[...] = st_c[...].reshape(128, 128).T

    def logit_grads(pair, _):
        column = (lax.broadcasted_iota(I32, (16, vocab), 1) + first_column).astype(F32)
        info = t_col[pl.ds(pl.multiple_of(pair * 16, 16), 16), :]
        for j in range(8):
            kind, x = j % 2, j // 2
            value = info[:, 16 * j : 16 * j + 1] * e_all[j, pair].astype(F32)
            value = jnp.where(column == info[:, 16 * j + 2 : 16 * j + 3], info[:, 16 * j + 1 : 16 * j + 2], value)
            g[kind, 2 * pair + x // 2, 16 * (x % 2) : 16 * (x % 2) + 16, :] = value.astype(BF16)
        return 0

    lax.fori_loop(0, 4, logit_grads, 0)

    def weight_tile(n, _):
        lanes = pl.ds(pl.multiple_of(n * 256, 256), 256)
        part = lax.dot_general(
            hid[:, :, :, lanes].reshape(512, 256), g[...].reshape(512, vocab), (((0,), (0,)), ((), ())),
            preferred_element_type=F32,
        )
        gw_ref[lanes, :] = part.astype(BF16)
        return 0

    lax.fori_loop(0, 4, weight_tile, 0)

    finished = sends[:-14]
    for c in finished:
        c.wait_send()
    halves = []
    for kind in (0, 1):
        for d in FAR_FIRST:
            arrived(r2.at[kind, d], d2_rs.at[kind, d], along(kind, 1))
        halves.append(s2[kind, me[1 - kind]].astype(F32) + sum(r2[kind, d].astype(F32) for d in range(1, 8)))
    gh_ref[...] = unpack(*halves).astype(BF16)

    for c in sends[-14:]:
        c.wait_send()


def body(hidden_states, weight, targets, upstream):
    vmem = pl.BlockSpec(memory_space=pltpu.VMEM)
    hbm = pl.BlockSpec(memory_space=pltpu.HBM)
    dma = pltpu.SemaphoreType.DMA
    scratch = [
        pltpu.VMEM((1024, 1024), BF16),
        pltpu.VMEM((1024, 1024), BF16),
        pltpu.VMEM((8, 1024), BF16),
        pltpu.VMEM((1, 512), I32),
        pltpu.VMEM((512,), BF16),
        pltpu.VMEM((2, 8, 32, 1024), BF16),
        pltpu.VMEM((2, 16, 256), BF16),
        pltpu.VMEM((2, 8, 16, 256), BF16),
        pltpu.VMEM((4, 64, 1024), F32),
        pltpu.VMEM((4, 64, 1024), F32),
        pltpu.VMEM((4, 64, 1024), F32),
        pltpu.VMEM((4, 64, 1024), F32),
        pltpu.VMEM((4, 3, 16, 1024), F32),
        pltpu.VMEM((8, 4, 16, 1024), BF16),
        pltpu.VMEM((2, 8, 32, 1024), BF16),
        pltpu.VMEM((2, 8, 32, 1024), BF16),
        pltpu.VMEM((2, 8, 32, 1024), BF16),
        pltpu.VMEM((2, 8, 16, 256), BF16),
        pltpu.VMEM((2, 8, 16, 256), BF16),
        pltpu.VMEM((2, 8, 32, 1024), BF16),
        pltpu.VMEM((2, 4, 32, 1024), BF16),
        pltpu.VMEM((2, 2, 32, 1024), BF16),
        pltpu.VMEM((2, 2, 16, 1024), BF16),
        pltpu.VMEM((128, 128), F32),
        pltpu.VMEM((512, 128), F32),
        pltpu.VMEM((128, 128), F32),
        pltpu.VMEM((8, 8, 128), F32),
        pltpu.VMEM((8, 8, 128), F32),
        pltpu.VMEM((8, 16, 128), F32),
        pltpu.VMEM((128, 128), F32),
        pltpu.VMEM((128, 128), F32),
        dma, dma((3,)),
        dma((2, 8)), dma((2, 8)), dma((2, 8)), dma((2, 8)), dma((2, 2)),
        dma((4,)), dma((4,)), dma((4, 3)), dma((4, 3)),
        dma((7, 4)), dma((8, 4)),
        dma((8,)), dma((8,)), dma((8,)), dma((8,)), dma((7,)), dma((8,)),
        dma((2, 8)), dma((2, 8)), dma((2, 8)), dma((2, 8)), dma((2, 8)), dma((2, 8)),
    ]
    operands = [
        pltpu.with_memory_space_constraint(a, pltpu.HBM)
        for a in (hidden_states, weight, targets.reshape(1, 512), upstream)
    ]
    return pl.pallas_call(
        kernel,
        out_shape=(
            jax.ShapeDtypeStruct(hidden_states.shape, BF16),
            jax.ShapeDtypeStruct(weight.shape, BF16),
        ),
        in_specs=[hbm, hbm, hbm, hbm],
        out_specs=(vmem, vmem),
        scratch_shapes=scratch,
        name="projection_backward",
        cost_estimate=pl.CostEstimate(flops=3 * 2 * 512 * 1024 * 1024, bytes_accessed=5 << 20, transcendentals=1 << 16),
        compiler_params=pltpu.CompilerParams(collective_id=0, has_side_effects=True, vmem_limit_bytes=48 << 20),
    )(*operands)


def solution(mesh):
    return jax.shard_map(
        body,
        mesh=mesh,
        in_specs=(P(("gx", "gy"), "gz"), P("gz", ("gx", "gy")), P(), P()),
        out_specs=(P(("gx", "gy"), "gz"), P("gz", ("gx", "gy"))),
        check_vma=False,
    )
```

```python
import functools

import jax
import jax.numpy as jnp
from jax import lax
from jax.experimental import pallas as pl
from jax.experimental.pallas import tpu as pltpu
from jax.sharding import PartitionSpec as P

MESH = pl.DeviceIdType.MESH
F32, BF16, I32 = jnp.float32, jnp.bfloat16, jnp.int32
FAR_FIRST = (4, 3, 5, 2, 6, 1, 7)
GROUP = ((2, 0), (2, 1), (1, 0), (3, 0), (1, 1), (3, 1), (0, 1))


def remote(src, dst, send_sem, recv_sem, device):
    return pltpu.make_async_remote_copy(
        src_ref=src, dst_ref=dst, send_sem=send_sem, recv_sem=recv_sem, device_id=device, device_id_type=MESH
    )


def upper_rows(shape):
    return lax.broadcasted_iota(I32, shape, 0) < 4


def pack(a):
    q = [a[:, 256 * k : 256 * (k + 1)] for k in range(4)]
    t = [pltpu.roll(x, 4, 0) for x in q]
    first = upper_rows((8, 256))
    low = jnp.concatenate([jnp.where(first, q[0], t[1]), jnp.where(first, q[2], t[3])], axis=0)
    high = jnp.concatenate([jnp.where(first, t[0], q[1]), jnp.where(first, t[2], q[3])], axis=0)
    return low, high


def unpack(low, high):
    first = upper_rows((8, 256))
    parts = []
    for k in range(2):
        a, c = low[8 * k : 8 * k + 8], high[8 * k : 8 * k + 8]
        parts.append(jnp.where(first, a, pltpu.roll(c, 4, 0)))
        parts.append(jnp.where(first, pltpu.roll(a, 4, 0), c))
    return jnp.concatenate(parts, axis=1)


def rows_of(*rows):
    sub = lax.broadcasted_iota(I32, (8, 128), 0)
    out = jnp.zeros((8, 128), F32)
    for k, row in enumerate(rows):
        out = jnp.where(sub == k, jnp.broadcast_to(row, (8, 128)), out)
    return out


def combine(stats):
    peaks = [stats[k, 0:1, :] for k in range(stats.shape[0])]
    peak = functools.reduce(jnp.maximum, peaks)
    scale = [jnp.exp(p - peak) for p in peaks]
    total = sum(stats[k, 1:2, :] * scale[k] for k in range(stats.shape[0]))
    chosen = sum(stats[k, 2:3, :] * scale[k] for k in range(stats.shape[0]))
    return peak, total, chosen


def kernel(
    h_hbm, w_hbm, tgt_hbm, up_hbm, gh_ref, gw_ref,
    w, wt, h_ref, tgt_ref, up_ref, hid, a1s, a1r, keep, cs, cr, xs, xr, e_all, g, p, r1, s2, r2,
    tp, tr, tg, th, own_col, all_col, stat_col, st_a, st_b, st_c, t_col, d_col,
    w_sem, in_sem, a1_ss, a1_rs, a2_ss, a2_rs, a2_hs, c_ss, c_rs, x_ss, x_rs,
    e_ss, e_rs, sa_ss, sa_rs, sb_ss, sb_rs, sc_ss, sc_rs, t_ss, t_rs, d1_ss, d1_rs, d2_ss, d2_rs,
):
    z, y, gz = lax.axis_index("gx"), lax.axis_index("gy"), lax.axis_index("gz")
    xx, core = gz // 2, gz % 2
    vocab = w.shape[1]
    zp, yp = z // 2, y // 2
    first_column = (z * 8 + y) * vocab
    contract = (((1,), (1,)), ((), ()))
    me = (z, y)

    def along(kind, d):
        return (z, (y + d) % 8, gz) if kind == 0 else ((z + d) % 8, y, gz)

    def member(dx, flip):
        c = 1 - core if flip else core
        return ((xx + dx) % 4) * 2 + c

    load_w = pltpu.make_async_copy(w_hbm, w, w_sem)
    load_w.start()
    loads = [
        pltpu.make_async_copy(src, dst, in_sem.at[i])
        for i, (src, dst) in enumerate(((h_hbm, h_ref), (tgt_hbm, tgt_ref), (up_hbm, up_ref)))
    ]
    for c in loads:
        c.start()

    barrier = pltpu.get_barrier_semaphore()
    for d in FAR_FIRST:
        for kind in (0, 1):
            pl.semaphore_signal(barrier, inc=1, device_id=along(kind, d), device_id_type=MESH)
    for dx, flip in GROUP:
        pl.semaphore_signal(barrier, inc=1, device_id=(z, y, member(dx, flip)), device_id_type=MESH)

    for c in loads:
        c.wait()
    low, high = pack(h_ref[...].astype(F32))
    a1s[0] = low.astype(BF16)
    a1s[1] = high.astype(BF16)
    a1r[0, y] = low.astype(BF16)
    a1r[1, z] = high.astype(BF16)

    pl.semaphore_wait(barrier, 21)

    sends = []
    for d in FAR_FIRST:
        for kind in (0, 1):
            c = remote(a1s.at[kind], a1r.at[kind, me[1 - kind]], a1_ss.at[kind, d], a1_rs.at[kind, me[1 - kind]], along(kind, d))
            c.start()
            sends.append(c)

    def arrived(dst, sem, peer):
        remote(dst, dst, sem, sem, peer).wait_recv()

    k = lax.broadcasted_iota(I32, (128, 512), 0)
    t = lax.broadcasted_iota(I32, (128, 512), 1)
    block = 2 * (k >> 4) + xx // 2
    other = (xx % 2) * 4 + ((k >> 2) & 3)
    zt = jnp.where(core == 0, block, other)
    yt = jnp.where(core == 0, other, block)
    token = zt * 64 + yt * 8 + core * 4 + (k & 3)
    select = jnp.where((token == t) & (k < 64), 1.0, 0.0).astype(BF16)
    tgt = tgt_ref[...]
    sub = lax.broadcasted_iota(I32, (128, 512), 0)
    values = jnp.where(sub == 0, jnp.broadcast_to((tgt >> 8).astype(F32), (128, 512)), 0.0)
    values = jnp.where(sub == 1, jnp.broadcast_to((tgt & 255).astype(F32), (128, 512)), values)
    values = jnp.where(sub == 2, jnp.broadcast_to(up_ref[...].reshape(1, 512).astype(F32), (128, 512)), values).astype(BF16)
    own_col[...] = lax.dot_general(select, values, contract, preferred_element_type=F32)
    own_row = lax.dot_general(values, select, contract, preferred_element_type=F32)
    tgt_row = own_row[0:1, :] * 256.0 + own_row[1:2, :]
    up_row = own_row[2:3, :]
    stat_col[...] = jnp.zeros((128, 128), F32)
    row = lax.broadcasted_iota(I32, (512, 128), 0)
    first, second = (row >> 5) & 7, (row & 31) >> 2
    token = jnp.where(row < 256, first * 64 + second * 8, second * 64 + first * 8 + 4) + (row & 3)
    order = (token[:, 0:1] == lax.broadcasted_iota(I32, (512, 512), 1)).astype(F32).astype(BF16)
    all_col[...] = lax.dot_general(order, values, contract, preferred_element_type=F32)
    load_w.wait()

    def turn(n, _):
        lanes = pl.ds(pl.multiple_of(n * 256, 256), 256)
        wt[:, lanes] = w[lanes, :].T
        return 0

    lax.fori_loop(0, 4, turn, 0)

    def chosen_rows(b, _):
        info = all_col[pl.ds(pl.multiple_of(b * 128, 128), 128), :]
        target = info[:, 0:1] * 256.0 + info[:, 1:2]
        hit = ((lax.broadcasted_iota(I32, (128, vocab), 1) + first_column).astype(F32) == target).astype(F32)
        part = jnp.dot(hit.astype(BF16), wt[...], preferred_element_type=F32).astype(BF16)
        tp[b // 2, pl.ds((b % 2) * 4, 4)] = part.reshape(4, 32, 1024)
        return 0

    def send_chosen(kind, src, dst, i, d):
        c = remote(src, dst, t_ss.at[kind, i], t_rs.at[kind, i], along(1 - kind, d))
        c.start()
        sends.append(c)

    def spread_chosen():
        for kind in (0, 1):
            for h, d in enumerate((1, 7)):
                half = pl.ds(16 * h, 16)
                send_chosen(kind, tp.at[kind, (me[kind] + 4) % 8, half], th.at[kind, h], 4 + h, 2 * d)
                send_chosen(kind, tp.at[kind, (me[kind] + 3 * d) % 8], tg.at[kind, h], 2 + h, d)
                send_chosen(kind, tp.at[kind, (me[kind] + d) % 8], tr.at[kind, h], h, d)

    def join_chosen():
        for kind in (0, 1):
            for h, d in enumerate((1, 7)):
                arrived(tg.at[kind, h], t_rs.at[kind, 2 + h], along(1 - kind, 1))
                arrived(th.at[kind, h], t_rs.at[kind, 4 + h], along(1 - kind, 1))
                q = (me[kind] + 2 * d) % 8
                for b in (0, 1):
                    rows = pl.ds(16 * b, 16)
                    total = tp[kind, q, rows, :].astype(F32) + tg[kind, h, rows, :].astype(F32)
                    if b == h:
                        total = total + th[kind, h].astype(F32)
                    tp[kind, q, rows, :] = total.astype(BF16)
                send_chosen(kind, tp.at[kind, q], tr.at[kind, 2 + h], 6 + h, 2 * d)

    for kind in (0, 1):
        mine = me[1 - kind]
        for d in range(1, 8):
            src = (mine + d) % 8
            arrived(a1r.at[kind, src], a1_rs.at[kind, src], along(kind, 1))
        for b in range(2):
            rows = [
                unpack(a1r[kind, 4 * b + 2 * q].astype(F32), a1r[kind, 4 * b + 2 * q + 1].astype(F32)) for q in range(2)
            ]
            hid[kind, me[kind], 16 * b : 16 * b + 16, :] = jnp.concatenate(rows, axis=0).astype(BF16)
        for d in (2, 6, 1, 7):
            slot = hid.at[kind, me[kind]]
            c = remote(slot, slot, a2_ss.at[kind, d], a2_rs.at[kind, me[kind]], along(1 - kind, d))
            c.start()
            sends.append(c)

    lax.fori_loop(0, 4, chosen_rows, 0)

    def shift(s, parity):
        return (0, 2 * parity + 3, 5 - 2 * parity, 2)[s]

    def pair_of(kind, s):
        return (zp + shift(s, z % 2)) % 4 if kind == 0 else (yp + shift(s, y % 2)) % 4

    def own_pair(s):
        return jnp.where(core == 0, pair_of(0, s), pair_of(1, s))

    def other_pair(s):
        return jnp.where(core == 0, pair_of(1, s), pair_of(0, s))

    sibling = (z, y, member(0, 1))

    def relay():
        for kind in (0, 1):
            for h, d in enumerate((1, 7)):
                q = (me[kind] - 2 * d) % 8
                slot = hid.at[kind, q]
                arrived(slot, a2_rs.at[kind, q], along(1 - kind, 1))
                c = remote(slot, slot, a2_ss.at[kind, 3 + 2 * h], a2_rs.at[kind, q], along(1 - kind, d))
                c.start()
                sends.append(c)
                half = hid.at[kind, q, 16 * h : 16 * h + 16]
                c = remote(half, half, a2_ss.at[kind, 4 * h], a2_hs.at[kind, h], along(1 - kind, 2 * d))
                c.start()
                sends.append(c)

    def multiply(s):
        for kind in (0, 1):
            q = 2 * pair_of(kind, s) + 1 - me[kind] % 2
            arrived(hid.at[kind, q], a2_rs.at[kind, q], along(1 - kind, 1))
            if s == 3:
                q = (me[kind] + 4) % 8
                for h in (0, 1):
                    arrived(hid.at[kind, q, 16 * h : 16 * h + 16], a2_hs.at[kind, h], along(1 - kind, 1))
        mine, others = own_pair(s), other_pair(s)

        lhs = jnp.concatenate(
            [hid[core, pl.ds(2 * mine, 2)].reshape(64, 1024), hid[1 - core, pl.ds(2 * others, 2)].reshape(64, 1024)], axis=0
        )
        part = jnp.dot(lhs, w[...], preferred_element_type=F32)
        cs[s] = part[64:]
        c = remote(cs.at[s], cr.at[s], c_ss.at[s], c_rs.at[s], sibling)
        c.start()
        sends.append(c)
        keep[s] = part[:64]

    def pass_on(s):
        arrived(cr.at[s], c_rs.at[s], sibling)
        for dx in (2, 1, 3, 0):
            rows = pl.ds(pl.multiple_of((xx + dx) % 4 * 16, 16), 16)
            xs[s, rows, :] = keep[s, rows, :] + cr[s, rows, :]
            if dx:
                c = remote(
                    xs.at[s, rows], xr.at[s, dx - 1], x_ss.at[s, dx - 1], x_rs.at[s, dx - 1], (z, y, member(dx, 0))
                )
                c.start()
                sends.append(c)

    def finish(s):
        for dx in (2, 1, 3):
            arrived(xr.at[s, dx - 1], x_rs.at[s, dx - 1], sibling)
        pair = own_pair(s)
        logits = xs[s, pl.ds(pl.multiple_of(xx * 16, 16), 16), :] + xr[s, 0] + xr[s, 1] + xr[s, 2]
        rows = pl.ds(pl.multiple_of(pair * 16, 16), 16)
        info = own_col[rows, :]
        target = info[:, 0:1] * 256.0 + info[:, 1:2]
        column = lax.broadcasted_iota(I32, (16, vocab), 1) + first_column
        hit = column.astype(F32) == target
        peak = jnp.max(logits, axis=1, keepdims=True)
        value = jnp.exp(logits - peak)
        rest = jnp.where(hit, 0.0, value)
        e_all[gz, pair] = rest.astype(BF16)
        for dx in (2, 1, 3):
            share(gz, pair, s, dx, member(dx, 0))
        share(gz, pair, s, 0, member(0, 1))
        total = jnp.sum(rest, axis=1, keepdims=True)
        chosen = jnp.sum(jnp.where(hit, value, 0.0), axis=1, keepdims=True)
        lane = lax.broadcasted_iota(I32, (16, 128), 1)
        stat_col[rows, :] = jnp.where(lane == 0, peak, jnp.where(lane == 1, total, jnp.where(lane == 2, chosen, 0.0)))

    def share(j, pair, s, i, to):
        slot = e_all.at[j, pair]
        c = remote(slot, slot, e_ss.at[i, s], e_rs.at[j, pair], (z, y, to))
        c.start()
        sends.append(c)

    def forward(s):
        for dx in (1, 3, 2):
            j, pair = member(dx, 0), own_pair(s)
            arrived(e_all.at[j, pair], e_rs.at[j, pair], sibling)
            share(j, pair, s, 3 + dx, member(0, 1))

    def scatter(kind, s):
        pair = pair_of(kind, s)
        if s == 0:
            chunks = [4 * pair + 1 - me[kind]]
            r1[kind, me[kind]] = p[kind, me[kind]]
        else:
            chunks = [2 * pair, 2 * pair + 1]
        for i, q in enumerate(chunks):
            to = (q, y, gz) if kind == 0 else (z, q, gz)
            c = remote(
                p.at[kind, q], r1.at[kind, me[kind]], d1_ss.at[kind, 2 * s + i], d1_rs.at[kind, me[kind]], to
            )
            c.start()
            sends.append(c)

    def terms(s):
        pairs = (pair_of(0, s), pair_of(1, s))
        for dx in range(4):
            j, pair = member(dx, 1), other_pair(s)
            arrived(e_all.at[j, pair], e_rs.at[j, pair], sibling)
        lhs = jnp.concatenate([e_all[2 * x + kind, pairs[kind]] for kind in (0, 1) for x in range(4)], axis=0)
        part = jnp.dot(lhs, wt[...], preferred_element_type=F32).astype(BF16)
        for kind in (0, 1):
            p[kind, pl.ds(2 * pairs[kind], 2)] = part[64 * kind : 64 * kind + 64].reshape(2, 32, 1024)
            scatter(kind, s)

    def stat_peer(phase, d):
        over_z = core == phase
        return (jnp.where(over_z, (z + d) % 8, z), jnp.where(over_z, y, (y + d) % 8), gz)

    def give(buf, ss, rs, phase):
        for d in FAR_FIRST:
            c = remote(buf.at[0], buf.at[d], ss.at[d], rs.at[d], stat_peer(phase, d))
            c.start()
            sends.append(c)

    def take(buf, rs, phase):
        for d in FAR_FIRST:
            arrived(buf.at[d], rs.at[d], stat_peer(phase, d))
        return combine(buf[...])

    def stats_first():
        st_a[0] = stat_col[...].T[0:8, :]
        give(st_a, sa_ss, sa_rs, 0)

    def stats_second():
        st_b[0] = rows_of(*take(st_a, sa_rs, 0))
        give(st_b, sb_ss, sb_rs, 1)

    def stats_third():
        peak, total, chosen = take(st_b, sb_rs, 1)
        used = lax.broadcasted_iota(I32, (1, 128), 1) < 64
        scale = up_row / jnp.where(used, total + chosen, 1.0)
        factors = [scale * jnp.exp(st_a[d, 0:1, :] - peak) for d in range(8)]
        st_c[gz, 0:8] = rows_of(factors[0], -scale * total, tgt_row)
        st_c[gz, 8:16] = rows_of(*factors)
        for i, (dx, flip) in enumerate(GROUP):
            c = remote(st_c.at[gz], st_c.at[gz], sc_ss.at[i], sc_rs.at[gz], (z, y, member(dx, flip)))
            c.start()
            sends.append(c)

    relay()
    multiply(0)
    pass_on(0)
    multiply(1)
    pass_on(1)
    finish(0)
    multiply(2)
    pass_on(2)
    finish(1)
    forward(0)
    multiply(3)
    spread_chosen()
    pass_on(3)
    finish(2)
    terms(0)
    forward(1)
    terms(1)
    finish(3)
    stats_first()
    forward(2)
    join_chosen()
    terms(2)
    stats_second()
    forward(3)
    terms(3)

    stats_third()

    for kind in (0, 1):
        for i in (0, 1, 2, 3):
            arrived(tr.at[kind, i], t_rs.at[kind, (0, 1, 6, 7)[i]], along(1 - kind, 1))
        total = tp[kind, me[kind]].astype(F32)
        for i in range(4):
            total = total + tr[kind, i].astype(F32)
        tp[kind, me[kind]] = total.astype(BF16)

    for dx, flip in GROUP:
        j = member(dx, flip)
        arrived(st_c.at[j], sc_rs.at[j], sibling)

    owners = [4 * (me[kind] % 2) + 2 * h + kind for kind in (0, 1) for h in (0, 1)]
    d_col[...] = jnp.concatenate([st_c[j] for j in owners] + [jnp.zeros((64, 128), F32)], axis=0).T
    for kind in (0, 1):
        for d in range(1, 8):
            src = (me[kind] + d) % 8
            arrived(r1.at[kind, src], d1_rs.at[kind, src], along(1 - kind, 1))
        info = d_col[pl.ds(pl.multiple_of(me[kind] // 2 * 16, 16), 16), :]
        for b in range(2):
            first = 32 * kind + 16 * b
            rows = info[:, first + 1 : first + 2] * tp[kind, me[kind], 16 * b : 16 * b + 16, :].astype(F32)
            for d in range(8):
                part = r1[kind, (me[kind] + 8 - d) % 8, 16 * b : 16 * b + 16, :].astype(F32)
                rows = rows + info[:, first + 8 + d : first + 9 + d] * part
            for q in range(2):
                low, high = pack(rows[8 * q : 8 * q + 8])
                s2[kind, 4 * b + 2 * q] = low.astype(BF16)
                s2[kind, 4 * b + 2 * q + 1] = high.astype(BF16)
        for d in FAR_FIRST:
            to = (me[1 - kind] + d) % 8
            c = remote(s2.at[kind, to], r2.at[kind, d], d2_ss.at[kind, d], d2_rs.at[kind, d], along(kind, d))
            c.start()
            sends.append(c)

    t_col[...] = st_c[...].reshape(128, 128).T

    def logit_grads(pair, _):
        column = (lax.broadcasted_iota(I32, (16, vocab), 1) + first_column).astype(F32)
        info = t_col[pl.ds(pl.multiple_of(pair * 16, 16), 16), :]
        for j in range(8):
            kind, x = j % 2, j // 2
            value = info[:, 16 * j : 16 * j + 1] * e_all[j, pair].astype(F32)
            value = jnp.where(column == info[:, 16 * j + 2 : 16 * j + 3], info[:, 16 * j + 1 : 16 * j + 2], value)
            g[kind, 2 * pair + x // 2, 16 * (x % 2) : 16 * (x % 2) + 16, :] = value.astype(BF16)
        return 0

    lax.fori_loop(0, 4, logit_grads, 0)

    def weight_tile(n, _):
        lanes = pl.ds(pl.multiple_of(n * 256, 256), 256)
        part = lax.dot_general(
            hid[:, :, :, lanes].reshape(512, 256), g[...].reshape(512, vocab), (((0,), (0,)), ((), ())),
            preferred_element_type=F32,
        )
        gw_ref[lanes, :] = part.astype(BF16)
        return 0

    lax.fori_loop(0, 4, weight_tile, 0)

    finished = sends[:-14]
    for c in finished:
        c.wait_send()
    halves = []
    for kind in (0, 1):
        for d in FAR_FIRST:
            arrived(r2.at[kind, d], d2_rs.at[kind, d], along(kind, 1))
        halves.append(s2[kind, me[1 - kind]].astype(F32) + sum(r2[kind, d].astype(F32) for d in range(1, 8)))
    gh_ref[...] = unpack(*halves).astype(BF16)

    for c in sends[-14:]:
        c.wait_send()


def body(hidden_states, weight, targets, upstream):
    vmem = pl.BlockSpec(memory_space=pltpu.VMEM)
    hbm = pl.BlockSpec(memory_space=pltpu.HBM)
    dma = pltpu.SemaphoreType.DMA
    scratch = [
        pltpu.VMEM((1024, 1024), BF16),
        pltpu.VMEM((1024, 1024), BF16),
        pltpu.VMEM((8, 1024), BF16),
        pltpu.VMEM((1, 512), I32),
        pltpu.VMEM((512,), BF16),
        pltpu.VMEM((2, 8, 32, 1024), BF16),
        pltpu.VMEM((2, 16, 256), BF16),
        pltpu.VMEM((2, 8, 16, 256), BF16),
        pltpu.VMEM((4, 64, 1024), F32),
        pltpu.VMEM((4, 64, 1024), F32),
        pltpu.VMEM((4, 64, 1024), F32),
        pltpu.VMEM((4, 64, 1024), F32),
        pltpu.VMEM((4, 3, 16, 1024), F32),
        pltpu.VMEM((8, 4, 16, 1024), BF16),
        pltpu.VMEM((2, 8, 32, 1024), BF16),
        pltpu.VMEM((2, 8, 32, 1024), BF16),
        pltpu.VMEM((2, 8, 32, 1024), BF16),
        pltpu.VMEM((2, 8, 16, 256), BF16),
        pltpu.VMEM((2, 8, 16, 256), BF16),
        pltpu.VMEM((2, 8, 32, 1024), BF16),
        pltpu.VMEM((2, 4, 32, 1024), BF16),
        pltpu.VMEM((2, 2, 32, 1024), BF16),
        pltpu.VMEM((2, 2, 16, 1024), BF16),
        pltpu.VMEM((128, 128), F32),
        pltpu.VMEM((512, 128), F32),
        pltpu.VMEM((128, 128), F32),
        pltpu.VMEM((8, 8, 128), F32),
        pltpu.VMEM((8, 8, 128), F32),
        pltpu.VMEM((8, 16, 128), F32),
        pltpu.VMEM((128, 128), F32),
        pltpu.VMEM((128, 128), F32),
        dma, dma((3,)),
        dma((2, 8)), dma((2, 8)), dma((2, 8)), dma((2, 8)), dma((2, 2)),
        dma((4,)), dma((4,)), dma((4, 3)), dma((4, 3)),
        dma((7, 4)), dma((8, 4)),
        dma((8,)), dma((8,)), dma((8,)), dma((8,)), dma((7,)), dma((8,)),
        dma((2, 8)), dma((2, 8)), dma((2, 8)), dma((2, 8)), dma((2, 8)), dma((2, 8)),
    ]
    operands = [
        pltpu.with_memory_space_constraint(a, pltpu.HBM)
        for a in (hidden_states, weight, targets.reshape(1, 512), upstream)
    ]
    return pl.pallas_call(
        kernel,
        out_shape=(
            jax.ShapeDtypeStruct(hidden_states.shape, BF16),
            jax.ShapeDtypeStruct(weight.shape, BF16),
        ),
        in_specs=[hbm, hbm, hbm, hbm],
        out_specs=(vmem, vmem),
        scratch_shapes=scratch,
        name="projection_backward",
        cost_estimate=pl.CostEstimate(flops=3 * 2 * 512 * 1024 * 1024, bytes_accessed=5 << 20, transcendentals=1 << 16),
        compiler_params=pltpu.CompilerParams(collective_id=0, has_side_effects=True, vmem_limit_bytes=48 << 20),
    )(*operands)


def solution(mesh):
    return jax.shard_map(
        body,
        mesh=mesh,
        in_specs=(P(("gx", "gy"), "gz"), P("gz", ("gx", "gy")), P(), P()),
        out_specs=(P(("gx", "gy"), "gz"), P("gz", ("gx", "gy"))),
        check_vma=False,
    )
```
